256 devices in a mesh: view: 2 (over core), dom: 128 (over y, x, z).
Axes of the slice: x: 4, y: 4, z: 8, core: 2. Of those that a mesh axis runs over, the one named last changes fastest.
Arguments:
- features: bfloat16 [2, 131072, 256], P('view', 'dom'), may hold values from -6 to 6
- local_adjacency: bfloat16 [2, 131072, 1024], P('view', 'dom'), may hold values from -0.1875 to 0.1875
- tile_keep: int32 [2, 1024, 8], P('view', 'dom'), may hold values 0 or 1
- halo_adjacency: bfloat16 [2, 131072, 1024], P('view', 'dom'), may hold values from -0.1875 to 0.1875
- send_rows: int32 [2, 16384, 8], P('view', 'dom'), may hold values from 0 to 1023
- send_count: int32 [2, 16384], P('view', 'dom'), may hold values from 1 to 8, as said below
- target: bfloat16 [2, 131072, 256], P('view', 'dom'), may hold values from -6 to 6
- w_encoder: bfloat16 [256, 256], replicated, may hold values from -0.375 to 0.375
- b_encoder: float32 [256], replicated, may hold values from -3 to 3
- w_predict_in: bfloat16 [256, 512], replicated, may hold values from -0.375 to 0.375
- b_predict_in: float32 [512], replicated, may hold values from -3 to 3
- w_predict_out: bfloat16 [512, 256], replicated, may hold values from -0.25 to 0.25
Outputs:
- features_grad: bfloat16 [2, 131072, 256], P('view', 'dom')
- encoder_w_grad: float32 [256, 256], replicated
- encoder_b_grad: float32 [256], replicated
- predict_in_w_grad: float32 [256, 512], replicated
- predict_in_b_grad: float32 [512], replicated
- predict_out_w_grad: float32 [512, 256], replicated
The draws below stay inside these ranges and needn't reach their ends.
Inputs may be any that keep to these rules, and one draw needn't show every extreme that they name: `send_count`: some pairs of partitions fill all 8 slots in every draw.
All inputs are finite; a program needn't handle non-finite values. No bound on the sum of `tile_keep` on one device may be relied on, other than what follows from the above.
Results may differ from the reference program's by a relative error of at most 0.012.
Values may be sent and summed in bfloat16 or wider, within the bound.
A program may use at most 64 MiB of HBM per device.

```python
import jax
import jax.numpy as jnp
from jax import lax

HID = 256
EMB = 256
PH = 512
NODE_DEV = 1024
HALO = 8
NODES = 131072
HALO_ALL = 1024
N_DOM = 128


def draw_send_count(key, part):
    base = jax.random.randint(key, (2, N_DOM * N_DOM), 1, HALO + 1)
    filled = jnp.arange(N_DOM * N_DOM) % 5 == 0
    return jnp.where(filled[None, :], HALO, base).astype(jnp.int32)


def plant(result, key, low, high):
    index_at = [jax.random.randint(jax.random.fold_in(key, axis), (), 0, length) for axis, length in enumerate(result.shape)]
    longest = result.shape.index(max(result.shape))
    beside = index_at[:longest] + [(index_at[longest] + 1) % result.shape[longest]] + index_at[longest + 1:]
    return result.at[tuple(index_at)].set(low).at[tuple(beside)].set(high)


def block_levels(stream_key, dims, cuts, low, high):
    def one(dim, parts):
        heights = jax.random.uniform(jax.random.fold_in(jax.random.fold_in(stream_key, 6), dim), (parts,), jnp.float32, low / len(cuts), high / len(cuts))
        return jnp.repeat(jnp.exp(heights), dims[dim] // parts).reshape((-1,) + (1,) * (len(dims) - dim - 1))

    gain = one(*cuts[0])
    for cut in cuts[1:]:
        gain = gain * one(*cut)
    return gain


def centred(rng, extent, scale, most, pieces=(), kind=jnp.bfloat16):
    values = scale * jax.random.normal(rng, extent, jnp.float32)
    if pieces:
        values = values * block_levels(rng, extent, pieces, -0.22, 0.18)
    return jnp.clip(values, -most, most).astype(kind)


def setup_inputs(seed: int = 0) -> dict:
    keys = jax.random.split(jax.random.key(seed), 13)
    features = centred(keys[0], (2, NODES, HID), 1.0, 6.0, ((0, 2), (1, 128)))
    local_adjacency = centred(keys[1], (2, NODES, NODE_DEV), NODE_DEV ** -0.5, 0.1875, ((0, 2), (1, 128)))
    tile_keep = plant((jax.random.randint(keys[2], (2, NODES // 128, NODE_DEV // 128), 0, 4) < 3).astype(jnp.int32), jax.random.fold_in(keys[2], 1), 0, 1)
    halo_adjacency = centred(keys[3], (2, NODES, HALO_ALL), HALO_ALL ** -0.5, 0.1875, ((0, 2), (1, 128)))
    send_rows = plant(jax.random.randint(keys[4], (2, N_DOM * N_DOM, HALO), 0, NODE_DEV), jax.random.fold_in(keys[4], 1), 0, NODE_DEV - 1).astype(jnp.int32)
    send_count = draw_send_count(jax.random.fold_in(keys[12], 71), 0)
    target = centred(keys[6], (2, NODES, EMB), 1.0, 6.0, ((0, 2), (1, 128)))
    w_encoder = centred(keys[7], (HID, EMB), HID ** -0.5, 0.375)
    b_encoder = centred(keys[8], (EMB,), 0.5, 3.0, (), jnp.float32)
    w_predict_in = centred(keys[9], (EMB, PH), EMB ** -0.5, 0.375)
    b_predict_in = centred(keys[10], (PH,), 0.5, 3.0, (), jnp.float32)
    w_predict_out = centred(keys[11], (PH, EMB), PH ** -0.5, 0.25)
    return dict(features=features, local_adjacency=local_adjacency, tile_keep=tile_keep, halo_adjacency=halo_adjacency, send_rows=send_rows, send_count=send_count, target=target, w_encoder=w_encoder, b_encoder=b_encoder, w_predict_in=w_predict_in, b_predict_in=b_predict_in, w_predict_out=w_predict_out)


loss_scale = 64.0

def partition_pass(inputs, w_encoder, b_encoder, w_predict_in, b_predict_in, w_predict_out):
    own_rows, adjacency, keep_tiles, halo_weights, received, other_target = inputs
    blocks = adjacency.shape[0] // 128
    kept = (adjacency.reshape(blocks, 128, blocks, 128) * keep_tiles.astype(adjacency.dtype)[:, None, :, None]).reshape(adjacency.shape)
    flat_received = received.reshape(-1, own_rows.shape[1])
    aggregated = (jnp.dot(kept, own_rows, preferred_element_type=jnp.float32) + jnp.dot(halo_weights, flat_received, preferred_element_type=jnp.float32)).astype(jnp.bfloat16)
    pre_encoder = jnp.dot(aggregated, w_encoder, preferred_element_type=jnp.float32) + b_encoder
    embed_value, embed_back = jax.vjp(jax.nn.gelu, pre_encoder)
    embedding = embed_value.astype(jnp.bfloat16)
    pre_hidden = jnp.dot(embedding, w_predict_in, preferred_element_type=jnp.float32) + b_predict_in
    hidden_value, hidden_back = jax.vjp(jax.nn.gelu, pre_hidden)
    hidden = hidden_value.astype(jnp.bfloat16)
    prediction = jnp.dot(hidden, w_predict_out, preferred_element_type=jnp.float32)
    target_value = other_target.astype(jnp.float32)
    squares_p = lax.optimization_barrier(jnp.sum(prediction * prediction, axis=1, keepdims=True)) + 1e-06
    squares_t = lax.optimization_barrier(jnp.sum(target_value * target_value, axis=1, keepdims=True)) + 1e-06
    joint = jnp.sqrt(squares_p * squares_t)
    cosine = lax.optimization_barrier(jnp.sum(prediction * target_value, axis=1, keepdims=True)) / joint
    prediction_grad = (-2.0 * loss_scale * (target_value / joint - cosine * prediction / squares_p)).astype(jnp.bfloat16)
    grad_out = jnp.dot(hidden.T, prediction_grad, preferred_element_type=jnp.float32)
    hidden_grad = hidden_back(jnp.dot(prediction_grad, w_predict_out.T, preferred_element_type=jnp.float32))[0].astype(jnp.bfloat16)
    grad_in_bias = lax.optimization_barrier(jnp.sum(hidden_grad.astype(jnp.float32), axis=0))
    grad_in = jnp.dot(embedding.T, hidden_grad, preferred_element_type=jnp.float32)
    embedding_grad = embed_back(jnp.dot(hidden_grad, w_predict_in.T, preferred_element_type=jnp.float32))[0].astype(jnp.bfloat16)
    grad_enc_bias = lax.optimization_barrier(jnp.sum(embedding_grad.astype(jnp.float32), axis=0))
    grad_enc = jnp.dot(aggregated.T, embedding_grad, preferred_element_type=jnp.float32)
    aggregated_grad = jnp.dot(embedding_grad, w_encoder.T, preferred_element_type=jnp.float32).astype(jnp.bfloat16)
    local_grad = jnp.dot(kept.T, aggregated_grad, preferred_element_type=jnp.float32)
    received_grad = jnp.dot(halo_weights.T, aggregated_grad, preferred_element_type=jnp.float32).astype(jnp.bfloat16).reshape(received.shape)
    return (local_grad, received_grad, grad_enc, grad_enc_bias, grad_in, grad_in_bias, grad_out)

def reference(features, local_adjacency, tile_keep, halo_adjacency, send_rows, send_count, target, w_encoder, b_encoder, w_predict_in, b_predict_in, w_predict_out):
    blocks = NODE_DEV // 128
    grads_per_view = []
    totals = None
    for view_index in range(2):
        rows = send_rows[view_index].reshape(N_DOM, N_DOM, HALO)
        live = jnp.arange(HALO, dtype=jnp.int32)[None, None, :] < send_count[view_index].reshape(N_DOM, N_DOM)[:, :, None]
        global_rows = (jnp.arange(N_DOM, dtype=jnp.int32)[:, None, None] * NODE_DEV + rows).astype(jnp.int32)
        sent = jnp.where(live[..., None], features[view_index][global_rows], jnp.zeros((), features.dtype))
        received = jnp.transpose(sent, (1, 0, 2, 3))
        other_target = target[1 - view_index].reshape(N_DOM, NODE_DEV, EMB)

        def one_partition(inputs):
            return partition_pass(inputs, w_encoder, b_encoder, w_predict_in, b_predict_in, w_predict_out)
        results = lax.map(one_partition, (features[view_index].reshape(N_DOM, NODE_DEV, HID), local_adjacency[view_index].reshape(N_DOM, NODE_DEV, NODE_DEV), tile_keep[view_index].reshape(N_DOM, blocks, blocks), halo_adjacency[view_index].reshape(N_DOM, NODE_DEV, N_DOM * HALO), received, other_target))
        local_grad = results[0]
        returned = jnp.transpose(results[1], (1, 0, 2, 3))
        returned = jnp.where(live[..., None], returned.astype(jnp.float32), jnp.zeros((), jnp.float32))
        feature_grad = local_grad.reshape(NODES, HID).at[global_rows.reshape(-1)].add(returned.reshape(-1, HID))
        grads_per_view.append(feature_grad.astype(jnp.bfloat16))
        partial_value = tuple((lax.optimization_barrier(jnp.sum(item, axis=0)) for item in results[2:]))
        totals = partial_value if totals is None else tuple((first + second for first, second in zip(totals, partial_value)))
    factor = 1.0 / jnp.sqrt(jnp.float32(2 * NODES))
    grad_enc, grad_enc_bias, grad_in, grad_in_bias, grad_out = tuple((item * factor for item in totals))
    return (jnp.stack(grads_per_view), grad_enc, grad_enc_bias, grad_in, grad_in_bias, grad_out)
```

```python
import jax
import jax.numpy as jnp
from jax import lax
from jax.experimental import pallas as pl
from jax.experimental.pallas import tpu as pltpu
from jax.sharding import PartitionSpec as P

f32, bf16, i32 = jnp.float32, jnp.bfloat16, jnp.int32
NY, NX, NZ = 4, 4, 8
NODES, WIDE, PEERS, SLOTS = 1024, 256, 128, 8
ORDER = (2, 1, 3, 0)
MESH = pl.DeviceIdType.MESH
MAIN = 80
loss_scale = 64.0


def dot(a, b, ca=1, cb=0):
    return lax.dot_general(a, b, (((ca,), (cb,)), ((), ())), preferred_element_type=f32)


def iota(shape, dim):
    return lax.broadcasted_iota(i32, shape, dim)


def gelu_both(v):
    k = 0.7978845608028654
    c = 0.044715
    v2 = v * v
    h = 0.5 + 0.5 * jnp.tanh(v * (k + (k * c) * v2))
    value = v * h
    slope = h + value * (1.0 - h) * (2.0 * k + (6.0 * k * c) * v2)
    return value, slope


def pack(g):
    rows = g.shape[0] // 8
    left = g[:, :128].reshape(rows, 8, 128)
    right = g[:, 128:].reshape(rows, 8, 128)
    return jnp.concatenate([left, right], axis=1).astype(bf16)


def unpack(c):
    rows = c.shape[0]
    wide = c.astype(f32)
    left = wide[:, :8].reshape(rows * 8, 128)
    right = wide[:, 8:].reshape(rows * 8, 128)
    return jnp.concatenate([left, right], axis=1).astype(bf16)


def block(i, size=256):
    return pl.ds(pl.multiple_of(i * size, size), size)


def kernel(
    feat_hbm, adj_hbm, keep_ref, halo_hbm, rows_ref, count_ref, target_hbm,
    we_ref, be_ref, wi_ref, bi_ref, wo_ref,
    fg_ref, ew_ref, eb_ref, iw_ref, ib_ref, ow_ref,
    feat, adj, halo, other, adj_t, halo_t, sel,
    acc, aggr, emb, hid, pgrad, hgrad, egrad, agrad, back,
    o1, a1, b1, c1, o2, a2, b2, c2,
    gf, m1, n1, m2, n2, m3, n3, m4, n4, pf,
    lsem, tsem,
    zs1, zr1, xs1, xr1, ys1, yr1, zs2, zr2, xs2, xr2, ys2, yr2,
    rvs, rxs, rxr, rys, ryr, rzs, rzr, gys, gyr, gxs, gxr,
):
    v = lax.axis_index("view")
    d = lax.axis_index("dom")
    z = d % NZ
    x = (d // NZ) % NX
    y = d // (NZ * NX)

    def at_z(c):
        return (v, (y * NX + x) * NZ + (z + c) % NZ)

    def at_x(c):
        return (v, (y * NX + (x + c) % NX) * NZ + z)

    def at_y(c):
        return (v, (((y + c) % NY) * NX + x) * NZ + z)

    mate = (1 - v, d)

    barrier = pltpu.get_barrier_semaphore()
    pl.semaphore_signal(barrier, inc=1, device_id=mate, device_id_type=MESH)
    for c in range(1, NY):
        pl.semaphore_signal(barrier, inc=1, device_id=at_y(c), device_id_type=MESH)
    for c in range(1, NX):
        pl.semaphore_signal(barrier, inc=1, device_id=at_x(c), device_id_type=MESH)
    for c in range(1, NZ):
        pl.semaphore_signal(barrier, inc=1, device_id=at_z(c), device_id_type=MESH)

    loads = [
        pltpu.make_async_copy(src, dst, lsem.at[i])
        for i, (src, dst) in enumerate(((feat_hbm, feat), (adj_hbm, adj), (halo_hbm, halo)))
    ]
    for item in loads:
        item.start()

    def remote(src, dst, ssem, rsem, device):
        return pltpu.make_async_remote_copy(
            src_ref=src, dst_ref=dst, send_sem=ssem, recv_sem=rsem,
            device_id=device, device_id_type=MESH,
        )

    class Exchange:
        def __init__(self, o, a, b, c, zs, zr, xs, xr, ys, yr):
            self.o, self.a, self.b, self.c = o, a, b, c
            self.zs, self.zr, self.xs, self.xr, self.ys, self.yr = zs, zr, xs, xr, ys, yr

        def z_copy(self, cy, c, slot):
            return remote(
                self.o.at[cy, :, (z + c) % NZ], self.a.at[cy, slot],
                self.zs.at[cy, c], self.zr.at[cy, c], at_z(c),
            )

        def x_home(self, cy, slot):
            return self.c.at[y, slot] if cy == 0 else self.b.at[cy - 1, slot]

        def x_copy(self, cy, c, slot):
            return remote(
                self.a.at[cy, :, (x + c) % NX], self.x_home(cy, slot),
                self.xs.at[cy, c], self.xr.at[cy, c], at_x(c),
            )

        def y_copy(self, cy, slot):
            return remote(
                self.b.at[cy - 1], self.c.at[slot],
                self.ys.at[cy], self.yr.at[cy], at_y(cy),
            )

        def send_z(self, cy):
            @pl.loop(1, NZ)
            def _(c):
                self.z_copy(cy, c, z).start()

            self.a[cy, z] = self.o[cy, :, z]

        def z_to_x(self, cy):
            @pl.loop(1, NZ)
            def _(c):
                self.z_copy(cy, c, (z - c + NZ) % NZ).wait_recv()

            for c in range(1, NX):
                self.x_copy(cy, c, x).start()
            self.x_home(cy, x)[...] = self.a[cy, :, x]

        def x_to_y(self, cy):
            for c in range(1, NX):
                self.x_copy(cy, c, (x - c + NX) % NX).wait_recv()
            if cy:
                self.y_copy(cy, y).start()

        def arrived(self, cy):
            source = (y - cy + NY) % NY
            if cy:
                self.y_copy(cy, source).wait_recv()
            return source, unpack(self.c[source].reshape(NX * NZ, 16, 128))

        def finish(self):
            for cy in ORDER:
                @pl.loop(1, NZ)
                def _(c):
                    self.z_copy(cy, c, z).wait_send()

                for c in range(1, NX):
                    self.x_copy(cy, c, x).wait_send()
                if cy:
                    self.y_copy(cy, y).wait_send()

    first = Exchange(o1, a1, b1, c1, zs1, zr1, xs1, xr1, ys1, yr1)
    second = Exchange(o2, a2, b2, c2, zs2, zr2, xs2, xr2, ys2, yr2)

    masked = jnp.where(iota((SLOTS, PEERS), 0) < count_ref[...], rows_ref[...], -1)
    code = jnp.concatenate([(masked >> 5).astype(f32), (masked & 31).astype(f32)], axis=0).astype(bf16)

    def outgoing(cy):
        there = (y + cy) % NY
        place = iota((256, PEERS), 0) // 8 + there * (NX * NZ)
        spread = jnp.where(iota((256, PEERS), 1) == place, 1.0, 0.0).astype(bf16)
        parts = dot(spread, code, 1, 1)
        lane = iota((256, 16), 1)
        weight = jnp.where(
            (lane & 7) == (iota((256, 16), 0) & 7), jnp.where(lane < 8, 32.0, 1.0), 0.0
        )
        row = jnp.sum(parts * weight, axis=1, keepdims=True).astype(i32)
        hot = jnp.where(iota((256, NODES), 1) == row, 1.0, 0.0).astype(bf16)
        o1[cy] = pack(dot(hot, feat[...])).reshape(NX, NZ, 16, 128)

    loads[0].wait()
    outgoing(ORDER[0])
    pl.semaphore_wait(barrier, NZ + NX + NY - 2)
    first.send_z(ORDER[0])
    for cy in ORDER[1:]:
        outgoing(cy)
        first.send_z(cy)
    swap = remote(target_hbm, other, tsem.at[0], tsem.at[1], mate)
    swap.start()

    loads[1].wait()

    @pl.loop(0, 8)
    def _(i):
        for j in range(8):
            keep = keep_ref[i, j].astype(f32)
            tile = adj[block(i, 128), j * 128 : (j + 1) * 128].astype(f32)
            adj[block(i, 128), j * 128 : (j + 1) * 128] = (tile * keep).astype(bf16)

    @pl.loop(0, 4)
    def _(r):
        acc[block(r), :] = dot(adj[block(r), :], feat[...])

    first.z_to_x(2)
    loads[2].wait()

    def transpose(source, target):
        @pl.loop(0, 4)
        def _(r):
            for q in range(4):
                target[q * 256 : (q + 1) * 256, block(r)] = source[
                    block(r), q * 256 : (q + 1) * 256
                ].T

    transpose(halo, halo_t)
    first.z_to_x(1)
    first.x_to_y(2)
    transpose(adj, adj_t)
    first.z_to_x(3)
    first.x_to_y(1)

    spread = jnp.where(iota((PEERS, NODES), 1) // 8 == iota((PEERS, NODES), 0), 1.0, 0.0).astype(bf16)
    parts = dot(code, spread)
    slot = iota((16, NODES), 0)
    weight = jnp.where((slot & 7) == (iota((16, NODES), 1) & 7), jnp.where(slot < 8, 32.0, 1.0), 0.0)
    row = jnp.sum(parts * weight, axis=0, keepdims=True).astype(i32)

    @pl.loop(0, 4)
    def _(r):
        sel[block(r), :] = jnp.where(iota((256, NODES), 0) + r * 256 == row, 1.0, 0.0).astype(bf16)

    first.z_to_x(0)
    first.x_to_y(3)

    def gather_in(cy):
        source, rows = first.arrived(cy)

        @pl.loop(0, 4)
        def _(r):
            acc[block(r), :] += dot(halo[block(r), block(source)], rows)

    gather_in(2)
    gather_in(1)
    first.x_to_y(0)
    gather_in(0)
    gather_in(3)
    swap.wait_recv()

    @pl.loop(0, 4)
    def _(r):
        at = block(r)
        agg = acc[at, :].astype(bf16)
        aggr[at, :] = agg
        value, enc_slope = gelu_both(dot(agg, we_ref[...]) + be_ref[...])
        embed = value.astype(bf16)
        emb[at, :] = embed
        value, in_slope = gelu_both(dot(embed, wi_ref[...]) + bi_ref[...])
        hidden = value.astype(bf16)
        hid[at, :] = hidden
        pred = dot(hidden, wo_ref[...])
        goal = other[at, :].astype(f32)
        squares_p = jnp.sum(pred * pred, axis=1, keepdims=True) + 1e-06
        squares_t = jnp.sum(goal * goal, axis=1, keepdims=True) + 1e-06
        over = 1.0 / jnp.sqrt(squares_p * squares_t)
        cosine = jnp.sum(pred * goal, axis=1, keepdims=True) * over
        pg = (
            (-2.0 * loss_scale * over) * goal + (2.0 * loss_scale * cosine / squares_p) * pred
        ).astype(bf16)
        pgrad[at, :] = pg
        hg = (in_slope * dot(pg, wo_ref[...], 1, 1)).astype(bf16)
        hgrad[at, :] = hg
        eg = (enc_slope * dot(hg, wi_ref[...], 1, 1)).astype(bf16)
        egrad[at, :] = eg
        agrad[at, :] = dot(eg, we_ref[...], 1, 1).astype(bf16)

    for cy in ORDER:
        there = (y + cy) % NY
        o2[cy] = pack(dot(halo_t[block(there), :], agrad[...])).reshape(NX, NZ, 16, 128)
        second.send_z(cy)

    pairs = (
        (hid, 0, pgrad, 0), (hid, 1, pgrad, 0), (emb, 0, hgrad, 0), (emb, 0, hgrad, 1), (aggr, 0, egrad, 0),
    )
    for i, (left, lq, right, rq) in enumerate(pairs):
        grad = dot(
            left[:, lq * 256 : (lq + 1) * 256], right[:, rq * 256 : (rq + 1) * 256], 0, 0
        )
        gf[i * 512 : i * 512 + 256, :] = grad[:, :128]
        gf[i * 512 + 256 : (i + 1) * 512, :] = grad[:, 128:]
    enc_bias = jnp.sum(egrad[...].astype(f32), axis=0, keepdims=True)
    in_bias = jnp.sum(hgrad[...].astype(f32), axis=0, keepdims=True)
    bias = jnp.concatenate(
        [enc_bias[:, :128], enc_bias[:, 128:]]
        + [in_bias[:, q * 128 : (q + 1) * 128] for q in range(4)]
        + [jnp.zeros((10, 128), f32)],
        axis=0,
    )
    half = 16 * MAIN
    m1[:half, :] = gf[block(1 - v, half), :].astype(bf16)
    m1[half:, :] = bias.astype(bf16)
    across = remote(m1, n1, rvs.at[0], rvs.at[1], mate)
    across.start()

    second.z_to_x(2)

    @pl.loop(0, 4)
    def _(r):
        back[block(r), :] = dot(adj_t[block(r), :], agrad[...])

    across.wait_recv()
    bias = m1[half:, :].astype(f32) + n1[half:, :].astype(f32)

    part = 4 * MAIN
    own = gf[block(v, half), :] + n1[:half, :].astype(f32)
    for q in range(NX):
        m2[q, :part, :] = own[q * part : (q + 1) * part, :].astype(bf16)
        m2[q, part:, :] = bias.astype(bf16)

    def over_x(c, slot):
        return remote(m2.at[(x + c) % NX], n2.at[slot], rxs.at[c], rxr.at[c], at_x(c))

    for c in range(1, NX):
        over_x(c, x).start()
    n2[x] = m2[x]

    second.z_to_x(1)
    second.x_to_y(2)
    second.z_to_x(3)
    second.x_to_y(1)

    for c in range(1, NX):
        over_x(c, (x - c + NX) % NX).wait_recv()
    total = sum(n2[q].astype(f32) for q in range(NX))
    for q in range(NY):
        m3[q, :MAIN, :] = total[q * MAIN : (q + 1) * MAIN, :].astype(bf16)
        m3[q, MAIN:, :] = total[part:, :].astype(bf16)

    def over_y(c, slot):
        return remote(m3.at[(y + c) % NY], n3.at[slot], rys.at[c], ryr.at[c], at_y(c))

    for c in range(1, NY):
        over_y(c, y).start()
    n3[y] = m3[y]

    second.z_to_x(0)
    second.x_to_y(3)

    for c in range(1, NY):
        over_y(c, (y - c + NY) % NY).wait_recv()
    m4[...] = sum(n3[q].astype(f32) for q in range(NY)).astype(bf16)

    def over_z(c, slot):
        return remote(m4, n4.at[slot], rzs.at[c], rzr.at[c], at_z(c))

    @pl.loop(1, NZ)
    def _(c):
        over_z(c, z).start()

    n4[z] = m4[...]

    def scatter_in(cy):
        source, rows = second.arrived(cy)

        @pl.loop(0, 4)
        def _(r):
            back[block(r), :] += dot(sel[block(r), block(source)], rows)

    scatter_in(2)

    @pl.loop(1, NZ)
    def _(c):
        over_z(c, (z - c + NZ) % NZ).wait_recv()

    scale = 1.0 / (2.0 * NODES * PEERS) ** 0.5
    total = sum(n4[q].astype(f32) for q in range(NZ)) * scale
    pf[v, x, y] = total[:MAIN, :].astype(bf16)

    def share_y(c, slot):
        return remote(pf.at[v, x, y], pf.at[v, x, slot], gys.at[c], gyr.at[c], at_y(c))

    for c in range(1, NY):
        share_y(c, y).start()
    eb_ref[...] = jnp.concatenate([total[MAIN + q : MAIN + q + 1, :] for q in range(2)], axis=1)
    ib_ref[...] = jnp.concatenate([total[MAIN + 2 + q : MAIN + 3 + q, :] for q in range(4)], axis=1)

    scatter_in(1)
    second.x_to_y(0)
    scatter_in(0)

    for c in range(1, NY):
        share_y(c, (y - c + NY) % NY).wait_recv()

    def share_x(c, slot):
        return remote(pf.at[v, x], pf.at[v, slot], gxs.at[c], gxr.at[c], at_x(c))

    for c in range(1, NX):
        share_x(c, x).start()

    scatter_in(3)
    fg_ref[...] = back[...].astype(bf16)

    for c in range(1, NX):
        share_x(c, (x - c + NX) % NX).wait_recv()
    share = remote(pf.at[v], pf.at[v], rvs.at[2], rvs.at[3], mate)
    share.start()
    remote(pf.at[v], pf.at[1 - v], rvs.at[2], rvs.at[3], mate).wait_recv()

    flat = pf[...].reshape(2 * half, 128)
    for i in range(2):
        for q in range(2):
            at = i * 512 + q * 256
            ow_ref[i * 256 : (i + 1) * 256, q * 128 : (q + 1) * 128] = flat[at : at + 256].astype(f32)
            at += 1024
            col = i * 256 + q * 128
            iw_ref[:, col : col + 128] = flat[at : at + 256].astype(f32)
    for q in range(2):
        at = 2048 + q * 256
        ew_ref[:, q * 128 : (q + 1) * 128] = flat[at : at + 256].astype(f32)

    swap.wait_send()
    first.finish()
    second.finish()
    across.wait_send()
    for c in range(1, NX):
        over_x(c, x).wait_send()
        over_y(c, y).wait_send()
        share_y(c, y).wait_send()
        share_x(c, x).wait_send()

    @pl.loop(1, NZ)
    def _(c):
        over_z(c, z).wait_send()

    share.wait_send()


def local(
    features, local_adjacency, tile_keep, halo_adjacency, send_rows, send_count, target,
    w_encoder, b_encoder, w_predict_in, b_predict_in, w_predict_out,
):
    vmem = pl.BlockSpec(memory_space=pltpu.VMEM)
    anywhere = pl.BlockSpec(memory_space=pl.ANY)
    rows = jnp.swapaxes(send_rows[0], 0, 1)
    dma = pltpu.SemaphoreType.DMA
    v16 = lambda *shape: pltpu.VMEM(shape, bf16)
    v32 = lambda *shape: pltpu.VMEM(shape, f32)
    exchange = [
        v16(NY, NX, NZ, 16, 128), v16(NY, NZ, NX, 16, 128),
        v16(NY - 1, NX, NZ, 16, 128), v16(NY, NX, NZ, 16, 128),
    ]
    exchange_sems = [dma((NY, NZ)), dma((NY, NZ)), dma((NY, NX)), dma((NY, NX)), dma((NY,)), dma((NY,))]
    outs = pl.pallas_call(
        kernel,
        out_shape=(
            jax.ShapeDtypeStruct((NODES, WIDE), bf16),
            jax.ShapeDtypeStruct((WIDE, WIDE), f32),
            jax.ShapeDtypeStruct((1, WIDE), f32),
            jax.ShapeDtypeStruct((WIDE, 2 * WIDE), f32),
            jax.ShapeDtypeStruct((1, 2 * WIDE), f32),
            jax.ShapeDtypeStruct((2 * WIDE, WIDE), f32),
        ),
        in_specs=[
            anywhere, anywhere, pl.BlockSpec(memory_space=pltpu.SMEM), anywhere, vmem, vmem, anywhere,
            vmem, vmem, vmem, vmem, vmem,
        ],
        out_specs=(vmem,) * 6,
        scratch_shapes=[
            v16(NODES, WIDE), v16(NODES, NODES), v16(NODES, NODES), v16(NODES, WIDE),
            v16(NODES, NODES), v16(NODES, NODES), v16(NODES, NODES),
            v32(NODES, WIDE), v16(NODES, WIDE), v16(NODES, WIDE), v16(NODES, 2 * WIDE),
            v16(NODES, WIDE), v16(NODES, 2 * WIDE), v16(NODES, WIDE), v16(NODES, WIDE), v32(NODES, WIDE),
        ]
        + exchange + exchange
        + [
            v32(32 * MAIN, 128), v16(16 * MAIN + 16, 128), v16(16 * MAIN + 16, 128),
            v16(NX, 4 * MAIN + 16, 128), v16(NX, 4 * MAIN + 16, 128),
            v16(NY, MAIN + 16, 128), v16(NY, MAIN + 16, 128),
            v16(MAIN + 16, 128), v16(NZ, MAIN + 16, 128), v16(2, NX, NY, MAIN, 128),
            dma((3,)), dma((2,)),
        ]
        + exchange_sems + exchange_sems
        + [dma((4,)), dma((NX,)), dma((NX,)), dma((NY,)), dma((NY,)), dma((NZ,)), dma((NZ,)),
           dma((NY,)), dma((NY,)), dma((NX,)), dma((NX,))],
        compiler_params=pltpu.CompilerParams(
            collective_id=0, has_side_effects=True, vmem_limit_bytes=56 * 1024 * 1024
        ),
    )(
        features[0], local_adjacency[0], tile_keep[0], halo_adjacency[0], rows, send_count, target[0],
        w_encoder, b_encoder[None], w_predict_in, b_predict_in[None], w_predict_out,
    )
    feature_grad, enc, enc_bias, into, in_bias, out = outs
    return feature_grad[None], enc, enc_bias[0], into, in_bias[0], out


def solution(mesh):
    split = P("view", "dom", None)
    return jax.shard_map(
        local,
        mesh=mesh,
        in_specs=(split, split, split, split, split, P("view", "dom"), split, P(), P(), P(), P(), P()),
        out_specs=(split, P(), P(), P(), P(), P()),
        check_vma=False,
    )
```

```python
import jax
import jax.numpy as jnp
from jax import lax
from jax.experimental import pallas as pl
from jax.experimental.pallas import tpu as pltpu
from jax.sharding import PartitionSpec as P

f32, bf16, i32 = jnp.float32, jnp.bfloat16, jnp.int32
NY, NX, NZ = 4, 4, 8
NODES, WIDE, PEERS, SLOTS = 1024, 256, 128, 8
ORDER = (0, 2, 3, 1)
ROUTE = {0: "zx", 1: "zxy", 2: "yxz", 3: "yzx"}
MESH = pl.DeviceIdType.MESH
HALF = 1280
XF, YF, TINY = 48, 32, 16
loss_scale = 64.0


def dot(a, b, ca=1, cb=0):
    return lax.dot_general(a, b, (((ca,), (cb,)), ((), ())), preferred_element_type=f32)


def iota(shape, dim):
    return lax.broadcasted_iota(i32, shape, dim)


def gelu_both(v):
    k = 0.7978845608028654
    c = 0.044715
    v2 = v * v
    h = 0.5 + 0.5 * jnp.tanh(v * (k + (k * c) * v2))
    value = v * h
    slope = h + value * (1.0 - h) * (2.0 * k + (6.0 * k * c) * v2)
    return value, slope


def pack(g):
    rows = g.shape[0] // 8
    left = g[:, :128].reshape(rows, 8, 128)
    right = g[:, 128:].reshape(rows, 8, 128)
    return jnp.concatenate([left, right], axis=1).astype(bf16)


def unpack(c):
    rows = c.shape[0]
    wide = c.astype(f32)
    left = wide[:, :8].reshape(rows * 8, 128)
    right = wide[:, 8:].reshape(rows * 8, 128)
    return jnp.concatenate([left, right], axis=1).astype(bf16)


def block(i, size=256):
    return pl.ds(pl.multiple_of(i * size, size), size)


def kernel(
    feat_hbm, adj_hbm, keep_hbm, halo_hbm, rows_hbm, count_hbm, target_hbm,
    we_hbm, be_hbm, wi_hbm, bi_hbm, wo_hbm,
    fg_ref, pfa, pfb, tiny_ref,
    feat, adj, keep_ref, halo, rows_ref, count_ref, we_ref, be_ref, wi_ref, bi_ref, wo_ref,
    other, adj_t, halo_t, sel,
    acc, aggr, emb, hid, pgrad, hgrad, egrad, agrad, back,
    o1, p1, q1, c1, o2, p2, q2, c2,
    gf, m1, n1, ma, na, mb, nb, mc, nc, md, nd, me, ne, pz,
    lsem, tsem,
    zs1, zr1, xs1, xr1, ys1, yr1, zs2, zr2, xs2, xr2, ys2, yr2,
    vs, vr, gs, gr, hs, hr,
):
    v = lax.axis_index("view")
    d = lax.axis_index("dom")
    z = d % NZ
    x = (d // NZ) % NX
    y = d // (NZ * NX)

    def at_z(c):
        return (v, (y * NX + x) * NZ + (z + c) % NZ)

    def at_x(c):
        return (v, (y * NX + (x + c) % NX) * NZ + z)

    def at_y(c):
        return (v, (((y + c) % NY) * NX + x) * NZ + z)

    mate = (1 - v, d)

    barrier = pltpu.get_barrier_semaphore()
    pl.semaphore_signal(barrier, inc=1, device_id=mate, device_id_type=MESH)
    for c in range(1, NY):
        pl.semaphore_signal(barrier, inc=1, device_id=at_y(c), device_id_type=MESH)
    for c in range(1, NX):
        pl.semaphore_signal(barrier, inc=1, device_id=at_x(c), device_id_type=MESH)
    for c in range(1, NZ):
        pl.semaphore_signal(barrier, inc=1, device_id=at_z(c), device_id_type=MESH)

    loads = [
        pltpu.make_async_copy(src, dst, lsem.at[i])
        for i, (src, dst) in enumerate((
            (rows_hbm, rows_ref), (count_hbm, count_ref), (feat_hbm, feat),
            (keep_hbm, keep_ref), (adj_hbm, adj), (halo_hbm, halo),
            (we_hbm, we_ref), (be_hbm, be_ref), (wi_hbm, wi_ref), (bi_hbm, bi_ref), (wo_hbm, wo_ref),
        ))
    ]
    for item in loads:
        item.start()

    def remote(src, dst, ssem, rsem, device):
        return pltpu.make_async_remote_copy(
            src_ref=src, dst_ref=dst, send_sem=ssem, recv_sem=rsem,
            device_id=device, device_id_type=MESH,
        )

    class Exchange:
        def __init__(self, o, p, q, c, zs, zr, xs, xr, ys, yr):
            self.o, self.p, self.q, self.c = o, p, q, c
            self.zs, self.zr, self.xs, self.xr, self.ys, self.yr = zs, zr, xs, xr, ys, yr

        def held(self, cy, k, last):
            if k == len(ROUTE[cy]):
                return self.c.at[last]
            return (self.o.at[cy], self.p.at[cy], self.q.at[cy - 1] if cy else None)[k]

        def copy(self, cy, k, c, back):
            line = ROUTE[cy][k]
            source = (y - cy + NY) % NY
            if line == "y":
                last = source if back else y
                return remote(
                    self.held(cy, k, None), self.held(cy, k + 1, last), self.ys.at[cy], self.yr.at[cy], at_y(cy)
                )
            here, there = self.held(cy, k, None), self.held(cy, k + 1, source)
            if line == "z":
                slot = (z - c + NZ) % NZ if back else z
                return remote(
                    here.at[:, (z + c) % NZ], there.at[:, slot], self.zs.at[cy, c], self.zr.at[cy, c], at_z(c)
                )
            slot = (x - c + NX) % NX if back else x
            return remote(here.at[(x + c) % NX], there.at[slot], self.xs.at[cy, c], self.xr.at[cy, c], at_x(c))

        def each(self, cy, k, act):
            line = ROUTE[cy][k]
            if line == "y":
                act(cy)
            elif line == "x":
                for c in range(1, NX):
                    act(c)
            else:
                pl.loop(1, NZ)(act)

        def start(self, cy, k):
            self.each(cy, k, lambda c: self.copy(cy, k, c, False).start())
            line = ROUTE[cy][k]
            if line != "y":
                here, there = self.held(cy, k, None), self.held(cy, k + 1, (y - cy + NY) % NY)
                if line == "z":
                    there[:, z] = here[:, z]
                else:
                    there[x] = here[x]

        def wait(self, cy, k):
            self.each(cy, k, lambda c: self.copy(cy, k, c, True).wait_recv())

        def step(self, cy, k):
            self.wait(cy, k - 1)
            self.start(cy, k)

        def arrived(self, cy):
            self.wait(cy, len(ROUTE[cy]) - 1)
            source = (y - cy + NY) % NY
            return source, unpack(self.c[source].reshape(NX * NZ, 16, 128))

        def finish(self):
            for cy in ORDER:
                for k in range(len(ROUTE[cy])):
                    self.each(cy, k, lambda c: self.copy(cy, k, c, False).wait_send())

    first = Exchange(o1, p1, q1, c1, zs1, zr1, xs1, xr1, ys1, yr1)
    second = Exchange(o2, p2, q2, c2, zs2, zr2, xs2, xr2, ys2, yr2)

    loads[0].wait()
    loads[1].wait()

    masked = jnp.where(iota((SLOTS, PEERS), 0) < count_ref[...], rows_ref[...], -1)
    code = jnp.concatenate([(masked >> 5).astype(f32), (masked & 31).astype(f32)], axis=0).astype(bf16)

    def outgoing(cy):
        there = (y + cy) % NY
        place = iota((256, PEERS), 0) // 8 + there * (NX * NZ)
        spread = jnp.where(iota((256, PEERS), 1) == place, 1.0, 0.0).astype(bf16)
        parts = dot(spread, code, 1, 1)
        lane = iota((256, 16), 1)
        weight = jnp.where(
            (lane & 7) == (iota((256, 16), 0) & 7), jnp.where(lane < 8, 32.0, 1.0), 0.0
        )
        row = jnp.sum(parts * weight, axis=1, keepdims=True).astype(i32)
        hot = jnp.where(iota((256, NODES), 1) == row, 1.0, 0.0).astype(bf16)
        o1[cy] = pack(dot(hot, feat[...])).reshape(NX, NZ, 16, 128)

    loads[2].wait()
    outgoing(ORDER[0])
    pl.semaphore_wait(barrier, NZ + NX + NY - 2)
    first.start(ORDER[0], 0)
    for cy in ORDER[1:]:
        outgoing(cy)
        first.start(cy, 0)
    swap = remote(target_hbm, other, tsem.at[0], tsem.at[1], mate)
    swap.start()

    for item in loads[3:5]:
        item.wait()

    @pl.loop(0, 8)
    def _(i):
        for j in range(8):
            keep = keep_ref[i, j].astype(f32)
            tile = adj[block(i, 128), j * 128 : (j + 1) * 128].astype(f32)
            adj[block(i, 128), j * 128 : (j + 1) * 128] = (tile * keep).astype(bf16)

    first.step(3, 1)

    @pl.loop(0, 4)
    def _(r):
        acc[block(r), :] = dot(adj[block(r), :], feat[...])

    first.step(0, 1)
    loads[5].wait()

    def transpose(source, target):
        @pl.loop(0, 4)
        def _(r):
            for q in range(4):
                target[q * 256 : (q + 1) * 256, block(r)] = source[
                    block(r), q * 256 : (q + 1) * 256
                ].T

    transpose(halo, halo_t)
    first.step(2, 1)
    transpose(adj, adj_t)
    first.step(1, 1)

    spread = jnp.where(iota((PEERS, NODES), 1) // 8 == iota((PEERS, NODES), 0), 1.0, 0.0).astype(bf16)
    parts = dot(code, spread)
    slot = iota((16, NODES), 0)
    weight = jnp.where((slot & 7) == (iota((16, NODES), 1) & 7), jnp.where(slot < 8, 32.0, 1.0), 0.0)
    row = jnp.sum(parts * weight, axis=0, keepdims=True).astype(i32)

    @pl.loop(0, 4)
    def _(r):
        sel[block(r), :] = jnp.where(iota((256, NODES), 0) + r * 256 == row, 1.0, 0.0).astype(bf16)

    def gather_in(cy):
        source, rows = first.arrived(cy)

        @pl.loop(0, 4)
        def _(r):
            acc[block(r), :] += dot(halo[block(r), block(source)], rows)

    first.step(2, 2)
    gather_in(0)
    first.step(1, 2)
    first.step(3, 2)
    for item in loads[6:]:
        item.wait()
    swap.wait_recv()
    gather_in(1)
    gather_in(3)
    gather_in(2)

    @pl.loop(0, 4)
    def _(r):
        at = block(r)
        agg = acc[at, :].astype(bf16)
        aggr[at, :] = agg
        value, enc_slope = gelu_both(dot(agg, we_ref[...]) + be_ref[...])
        embed = value.astype(bf16)
        emb[at, :] = embed
        value, in_slope = gelu_both(dot(embed, wi_ref[...]) + bi_ref[...])
        hidden = value.astype(bf16)
        hid[at, :] = hidden
        pred = dot(hidden, wo_ref[...])
        goal = other[at, :].astype(f32)
        squares_p = jnp.sum(pred * pred, axis=1, keepdims=True) + 1e-06
        squares_t = jnp.sum(goal * goal, axis=1, keepdims=True) + 1e-06
        over = 1.0 / jnp.sqrt(squares_p * squares_t)
        cosine = jnp.sum(pred * goal, axis=1, keepdims=True) * over
        pg = (
            (-2.0 * loss_scale * over) * goal + (2.0 * loss_scale * cosine / squares_p) * pred
        ).astype(bf16)
        pgrad[at, :] = pg
        hg = (in_slope * dot(pg, wo_ref[...], 1, 1)).astype(bf16)
        hgrad[at, :] = hg
        eg = (enc_slope * dot(hg, wi_ref[...], 1, 1)).astype(bf16)
        egrad[at, :] = eg
        agrad[at, :] = dot(eg, we_ref[...], 1, 1).astype(bf16)

    for cy in ORDER:
        there = (y + cy) % NY
        o2[cy] = pack(dot(halo_t[block(there), :], agrad[...])).reshape(NX, NZ, 16, 128)
        second.start(cy, 0)

    pairs = (
        (hid, 0, pgrad, 0), (hid, 1, pgrad, 0), (emb, 0, hgrad, 0), (emb, 0, hgrad, 1), (aggr, 0, egrad, 0),
    )
    for i, (left, lq, right, rq) in enumerate(pairs):
        grad = dot(
            left[:, lq * 256 : (lq + 1) * 256], right[:, rq * 256 : (rq + 1) * 256], 0, 0
        )
        gf[i * 512 : i * 512 + 256, :] = grad[:, :128]
        gf[i * 512 + 256 : (i + 1) * 512, :] = grad[:, 128:]
    enc_bias = jnp.sum(egrad[...].astype(f32), axis=0, keepdims=True)
    in_bias = jnp.sum(hgrad[...].astype(f32), axis=0, keepdims=True)
    bias = jnp.concatenate(
        [enc_bias[:, :128], enc_bias[:, 128:]]
        + [in_bias[:, q * 128 : (q + 1) * 128] for q in range(4)]
        + [jnp.zeros((10, 128), f32)],
        axis=0,
    )
    m1[:HALF, :] = gf[block(1 - v, HALF), :].astype(bf16)
    m1[HALF:, :] = bias.astype(bf16)
    across = remote(m1, n1, vs.at[0], vr.at[0], mate)
    across.start()

    second.step(3, 1)
    second.step(0, 1)

    across.wait_recv()
    bias = m1[HALF:, :].astype(f32) + n1[HALF:, :].astype(f32)
    own = gf[block(v, HALF), :] + n1[:HALF, :].astype(f32)

    for q in range(4):
        ma[q] = own[q * 4 * XF : (q + 1) * 4 * XF, :].astype(bf16)
        at = 16 * XF + q * 4 * YF
        mb[q, : 4 * YF, :] = own[at : at + 4 * YF, :].astype(bf16)
        mb[q, 4 * YF :, :] = bias.astype(bf16)

    def over_x(k, src, dst, c, back=False):
        slot = (x - c + NX) % NX if back else x
        return remote(src.at[(x + c) % NX], dst.at[slot], gs.at[k, c], gr.at[k, c], at_x(c))

    def over_y(k, src, dst, c, back=False):
        slot = (y - c + NY) % NY if back else y
        return remote(src.at[(y + c) % NY], dst.at[slot], gs.at[k, c], gr.at[k, c], at_y(c))

    for c in (2, 1, 3):
        over_x(0, ma, na, c).start()
        over_y(1, mb, nb, c).start()
    na[x] = ma[x]
    nb[y] = mb[y]

    @pl.loop(0, 4)
    def _(r):
        back[block(r), :] = dot(adj_t[block(r), :], agrad[...])

    second.step(2, 1)
    second.step(1, 1)

    for c in range(1, 4):
        over_x(0, ma, na, c, True).wait_recv()
        over_y(1, mb, nb, c, True).wait_recv()
    total = sum(na[q].astype(f32) for q in range(NX))
    for q in range(NY):
        mc[q] = total[q * XF : (q + 1) * XF, :].astype(bf16)
    total = sum(nb[q].astype(f32) for q in range(NY))
    for q in range(NX):
        md[q, :YF, :] = total[q * YF : (q + 1) * YF, :].astype(bf16)
        md[q, YF:, :] = total[4 * YF :, :].astype(bf16)
    for c in (2, 1, 3):
        over_y(2, mc, nc, c).start()
        over_x(3, md, nd, c).start()
    nc[y] = mc[y]
    nd[x] = md[x]

    second.step(2, 2)

    def scatter_in(cy):
        source, rows = second.arrived(cy)

        @pl.loop(0, 4)
        def _(r):
            back[block(r), :] += dot(sel[block(r), block(source)], rows)

    scatter_in(0)

    for c in range(1, 4):
        over_y(2, mc, nc, c, True).wait_recv()
        over_x(3, md, nd, c, True).wait_recv()
    total = sum(nc[q].astype(f32) for q in range(NY)).astype(bf16)
    for q in range(3):
        me[q] = total[q * 16 : (q + 1) * 16, :]
    total = sum(nd[q].astype(f32) for q in range(NX)).astype(bf16)
    for q in range(3):
        me[3 + q] = total[q * 16 : (q + 1) * 16, :]
    me[6:] = jnp.zeros((2, 16, 128), bf16)

    def to_z(c, back=False):
        slot = (z - c + NZ) % NZ if back else z
        return remote(me.at[(z + c) % NZ], ne.at[slot], hs.at[0, c], hr.at[0, c], at_z(c))

    @pl.loop(1, NZ)
    def _(c):
        to_z(c).start()

    ne[z] = me[z]
    second.step(1, 2)
    second.step(3, 2)

    @pl.loop(1, NZ)
    def _(c):
        to_z(c, True).wait_recv()

    scale = 1.0 / (2.0 * NODES * PEERS) ** 0.5
    pz[z] = (sum(ne[q].astype(f32) for q in range(NZ)) * scale).astype(bf16)

    def from_z(c, back=False):
        slot = (z - c + NZ) % NZ if back else z
        return remote(pz.at[z], pz.at[slot], hs.at[1, c], hr.at[1, c], at_z(c))

    @pl.loop(1, NZ)
    def _(c):
        from_z(c).start()

    scatter_in(1)

    @pl.loop(1, NZ)
    def _(c):
        from_z(c, True).wait_recv()

    for q in range(3):
        pfa[v, x, y, q * 16 : (q + 1) * 16, :] = pz[q]
    for q in range(2):
        pfb[v, y, x, q * 16 : (q + 1) * 16, :] = pz[3 + q]
    tiny_ref[...] = pz[5].astype(f32)

    def share_y(k, src, dst, c, back=False):
        slot = (y - c + NY) % NY if back else y
        return remote(src(y), dst(slot), gs.at[k, c], gr.at[k, c], at_y(c))

    def share_x(k, src, dst, c, back=False):
        slot = (x - c + NX) % NX if back else x
        return remote(src(x), dst(slot), gs.at[k, c], gr.at[k, c], at_x(c))

    xy = lambda q: pfa.at[v, x, q]
    yx = lambda q: pfb.at[v, y, q]
    for c in (2, 1, 3):
        share_y(4, xy, xy, c).start()
        share_x(5, yx, yx, c).start()
    scatter_in(3)
    for c in range(1, 4):
        share_y(4, xy, xy, c, True).wait_recv()
        share_x(5, yx, yx, c, True).wait_recv()
    xs = lambda q: pfa.at[v, q]
    ys = lambda q: pfb.at[v, q]
    for c in (2, 1, 3):
        share_x(6, xs, xs, c).start()
        share_y(7, ys, ys, c).start()

    def pass_a(c):
        q = (x - c + NX) % NX
        return remote(pfa.at[v, q], pfa.at[v, q], vs.at[1 + c], vr.at[1 + c], mate)

    def pass_b(c):
        q = (y - c + NY) % NY
        return remote(pfb.at[v, q], pfb.at[v, q], vs.at[5 + c], vr.at[5 + c], mate)

    def taken_a(c):
        q = (x - c + NX) % NX
        return remote(pfa.at[v, q], pfa.at[1 - v, q], vs.at[1 + c], vr.at[1 + c], mate)

    def taken_b(c):
        q = (y - c + NY) % NY
        return remote(pfb.at[v, q], pfb.at[1 - v, q], vs.at[5 + c], vr.at[5 + c], mate)

    pass_a(0).start()
    pass_b(0).start()
    scatter_in(2)
    fg_ref[...] = back[...].astype(bf16)
    for c in (1, 3, 2):
        share_x(6, xs, xs, c, True).wait_recv()
        pass_a(c).start()
        share_y(7, ys, ys, c, True).wait_recv()
        pass_b(c).start()
    for c in range(4):
        taken_a(c).wait_recv()
        taken_b(c).wait_recv()

    swap.wait_send()
    first.finish()
    second.finish()
    across.wait_send()
    for c in range(1, 4):
        over_x(0, ma, na, c).wait_send()
        over_y(1, mb, nb, c).wait_send()
        over_y(2, mc, nc, c).wait_send()
        over_x(3, md, nd, c).wait_send()
        share_y(4, xy, xy, c).wait_send()
        share_x(5, yx, yx, c).wait_send()
        share_x(6, xs, xs, c).wait_send()
        share_y(7, ys, ys, c).wait_send()
    for c in range(4):
        pass_a(c).wait_send()
        pass_b(c).wait_send()

    @pl.loop(1, NZ)
    def _(c):
        to_z(c).wait_send()
        from_z(c).wait_send()


def results(fg_in, pfa, pfb, tiny, fg_ref, ew_ref, eb_ref, iw_ref, ib_ref, ow_ref, sem):
    move = pltpu.make_async_copy(fg_in, fg_ref, sem)
    move.start()

    def rows(i):
        view, r = i // 5, i % 5
        src, at = (pfa, r * 256) if r < 3 else (pfb, (r - 3) * 256)
        return src[view, at : at + 256, :].astype(f32)

    for i in range(2):
        for q in range(2):
            ow_ref[i * 256 : (i + 1) * 256, q * 128 : (q + 1) * 128] = rows(2 * i + q)
            col = i * 256 + q * 128
            iw_ref[:, col : col + 128] = rows(4 + 2 * i + q)
    for q in range(2):
        ew_ref[:, q * 128 : (q + 1) * 128] = rows(8 + q)
        eb_ref[:, q * 128 : (q + 1) * 128] = tiny[q : q + 1, :]
    for q in range(4):
        ib_ref[:, q * 128 : (q + 1) * 128] = tiny[2 + q : 3 + q, :]
    move.wait()


def local(
    features, local_adjacency, tile_keep, halo_adjacency, send_rows, send_count, target,
    w_encoder, b_encoder, w_predict_in, b_predict_in, w_predict_out,
):
    vmem = pl.BlockSpec(memory_space=pltpu.VMEM)
    anywhere = pl.BlockSpec(memory_space=pl.ANY)
    dma = pltpu.SemaphoreType.DMA
    v16 = lambda *shape: pltpu.VMEM(shape, bf16)
    v32 = lambda *shape: pltpu.VMEM(shape, f32)
    exchange = [v16(NY, NX, NZ, 16, 128), v16(NY, NX, NZ, 16, 128), v16(NY - 1, NX, NZ, 16, 128), v16(NY, NX, NZ, 16, 128)]
    exchange_sems = [dma((NY, NZ)), dma((NY, NZ)), dma((NY, NX)), dma((NY, NX)), dma((NY,)), dma((NY,))]
    feature_grad, pfa, pfb, tiny = pl.pallas_call(
        kernel,
        out_shape=(
            jax.ShapeDtypeStruct((NODES, WIDE), bf16),
            jax.ShapeDtypeStruct((2, NX, NY, XF, 128), bf16),
            jax.ShapeDtypeStruct((2, NY, NX, YF, 128), bf16),
            jax.ShapeDtypeStruct((TINY, 128), f32),
        ),
        in_specs=[anywhere] * 12,
        out_specs=(vmem,) * 4,
        scratch_shapes=[
            v16(NODES, WIDE), v16(NODES, NODES), pltpu.SMEM((8, 8), i32), v16(NODES, NODES),
            pltpu.VMEM((SLOTS, PEERS), i32), pltpu.VMEM((1, PEERS), i32),
            v16(WIDE, WIDE), v32(1, WIDE), v16(WIDE, 2 * WIDE), v32(1, 2 * WIDE), v16(2 * WIDE, WIDE),
            v16(NODES, WIDE), v16(NODES, NODES), v16(NODES, NODES), v16(NODES, NODES),
            v32(NODES, WIDE), v16(NODES, WIDE), v16(NODES, WIDE), v16(NODES, 2 * WIDE),
            v16(NODES, WIDE), v16(NODES, 2 * WIDE), v16(NODES, WIDE), v16(NODES, WIDE), v32(NODES, WIDE),
        ]
        + exchange + exchange
        + [
            v32(2 * HALF, 128), v16(HALF + TINY, 128), v16(HALF + TINY, 128),
            v16(NX, 4 * XF, 128), v16(NX, 4 * XF, 128),
            v16(NY, 4 * YF + TINY, 128), v16(NY, 4 * YF + TINY, 128),
            v16(NY, XF, 128), v16(NY, XF, 128), v16(NX, YF + TINY, 128), v16(NX, YF + TINY, 128),
            v16(NZ, 16, 128), v16(NZ, 16, 128), v16(NZ, 16, 128),
            dma((11,)), dma((2,)),
        ]
        + exchange_sems + exchange_sems
        + [dma((9,)), dma((9,)), dma((8, 4)), dma((8, 4)), dma((2, NZ)), dma((2, NZ))],
        compiler_params=pltpu.CompilerParams(
            collective_id=0, has_side_effects=True, vmem_limit_bytes=48 * 1024 * 1024
        ),
    )(
        features[0], local_adjacency[0], tile_keep[0], halo_adjacency[0],
        jnp.swapaxes(send_rows[0], 0, 1), send_count, target[0],
        w_encoder, b_encoder[None], w_predict_in, b_predict_in[None], w_predict_out,
    )
    feature_grad, enc, enc_bias, into, in_bias, out = pl.pallas_call(
        results,
        out_shape=(
            jax.ShapeDtypeStruct((NODES, WIDE), bf16),
            jax.ShapeDtypeStruct((WIDE, WIDE), f32),
            jax.ShapeDtypeStruct((1, WIDE), f32),
            jax.ShapeDtypeStruct((WIDE, 2 * WIDE), f32),
            jax.ShapeDtypeStruct((1, 2 * WIDE), f32),
            jax.ShapeDtypeStruct((2 * WIDE, WIDE), f32),
        ),
        in_specs=[anywhere, vmem, vmem, vmem],
        out_specs=(anywhere,) + (vmem,) * 5,
        scratch_shapes=[pltpu.SemaphoreType.DMA(())],
    )(
        feature_grad, pfa.reshape(2, 16 * XF, 128), pfb.reshape(2, 16 * YF, 128), tiny
    )
    return feature_grad[None], enc, enc_bias[0], into, in_bias[0], out


def solution(mesh):
    split = P("view", "dom", None)
    return jax.shard_map(
        local,
        mesh=mesh,
        in_specs=(split, split, split, split, split, P("view", "dom"), split, P(), P(), P(), P(), P()),
        out_specs=(split, P(), P(), P(), P(), P()),
        check_vma=False,
    )
```

```python
import jax
import jax.numpy as jnp
from jax import lax
from jax.experimental import pallas as pl
from jax.experimental.pallas import tpu as pltpu
from jax.sharding import PartitionSpec as P

f32, bf16, i32 = jnp.float32, jnp.bfloat16, jnp.int32
NY, NX, NZ = 4, 4, 8
NODES, WIDE, PEERS, SLOTS = 1024, 256, 128, 8
ORDER = (2, 1, 3, 0)
MESH = pl.DeviceIdType.MESH
PLANE = NX * NZ
HALF, PART, TINY = 1280, 80, 16
loss_scale = 64.0


def dot(a, b, ca=1, cb=0):
    return lax.dot_general(a, b, (((ca,), (cb,)), ((), ())), preferred_element_type=f32)


def iota(shape, dim):
    return lax.broadcasted_iota(i32, shape, dim)


def gelu_both(v):
    k = 0.7978845608028654
    c = 0.044715
    v2 = v * v
    h = 0.5 + 0.5 * jnp.tanh(v * (k + (k * c) * v2))
    value = v * h
    slope = h + value * (1.0 - h) * (2.0 * k + (6.0 * k * c) * v2)
    return value, slope


def pack(g):
    rows = g.shape[0] // 8
    left = g[:, :128].reshape(rows, 8, 128)
    right = g[:, 128:].reshape(rows, 8, 128)
    return jnp.concatenate([left, right], axis=1).astype(bf16)


def unpack(c):
    rows = c.shape[0]
    wide = c.astype(f32)
    left = wide[:, :8].reshape(rows * 8, 128)
    right = wide[:, 8:].reshape(rows * 8, 128)
    return jnp.concatenate([left, right], axis=1).astype(bf16)


def block(i, size=256):
    return pl.ds(pl.multiple_of(i * size, size), size)


def kernel(
    feat_hbm, adj_hbm, keep_hbm, halo_hbm, rows_hbm, count_hbm, target_hbm,
    we_hbm, be_hbm, wi_hbm, bi_hbm, wo_hbm,
    fg_ref, pf, tiny_ref,
    feat, adj, keep_ref, halo, rows_ref, count_ref, we_ref, be_ref, wi_ref, bi_ref, wo_ref,
    other, adj_t, halo_t, sel,
    acc, aggr, emb, hid, pgrad, hgrad, egrad, agrad, back,
    o1, c1, o2, c2,
    gf, m1, n1, ma, na, me, ne, pz,
    lsem, tsem, x_in, y_in,
    es1, er1, es2, er2, vs, vr, ps, pr, hs, hr,
):
    v = lax.axis_index("view")
    d = lax.axis_index("dom")
    z = d % NZ
    x = (d // NZ) % NX
    y = d // (NZ * NX)

    def at_z(c):
        return (v, (y * NX + x) * NZ + (z + c) % NZ)

    def at_x(c):
        return (v, (y * NX + (x + c) % NX) * NZ + z)

    def at_y(c):
        return (v, (((y + c) % NY) * NX + x) * NZ + z)

    def at_plane(c):
        return (v, (d + c * NZ) % PEERS)

    mate = (1 - v, d)

    barrier = pltpu.get_barrier_semaphore()
    pl.semaphore_signal(barrier, inc=1, device_id=mate, device_id_type=MESH)
    for c in range(1, NY):
        pl.semaphore_signal(barrier, inc=1, device_id=at_y(c), device_id_type=MESH)
    for c in range(1, NX):
        pl.semaphore_signal(barrier, inc=1, device_id=at_x(c), device_id_type=MESH)
    for c in range(1, NZ):
        pl.semaphore_signal(barrier, inc=1, device_id=at_z(c), device_id_type=MESH)

    loads = [
        pltpu.make_async_copy(src, dst, lsem.at[i])
        for i, (src, dst) in enumerate((
            (rows_hbm, rows_ref), (count_hbm, count_ref), (feat_hbm, feat),
            (keep_hbm, keep_ref), (adj_hbm, adj), (halo_hbm, halo),
            (we_hbm, we_ref), (be_hbm, be_ref), (wi_hbm, wi_ref), (bi_hbm, bi_ref), (wo_hbm, wo_ref),
        ))
    ]
    for item in loads:
        item.start()

    def remote(src, dst, ssem, rsem, device):
        return pltpu.make_async_remote_copy(
            src_ref=src, dst_ref=dst, send_sem=ssem, recv_sem=rsem,
            device_id=device, device_id_type=MESH,
        )

    class Exchange:
        def __init__(self, o, c, ss, rs):
            self.o, self.c, self.ss, self.rs = o, c, ss, rs

        def start(self, cy):
            there = (y + cy) % NY
            here = d % PLANE

            @pl.loop(0 if cy else 1, PLANE)
            def _(i):
                j = (here + i) % PLANE
                remote(
                    self.o.at[cy, j], self.c.at[y, here], self.ss.at[cy], self.rs.at[cy], (v, there * PLANE + j)
                ).start()

            if cy == 0:
                self.c[y, here] = self.o[0, here]

        def whole(self, cy):
            source = (y - cy + NY) % NY
            n = PLANE if cy else PLANE - 1
            return remote(
                self.o.at[cy, pl.ds(0, n)], self.c.at[source, pl.ds(0, n)], self.ss.at[cy], self.rs.at[cy], at_y(cy or 1)
            )

        def arrived(self, cy):
            self.whole(cy).wait_recv()
            source = (y - cy + NY) % NY
            return source, unpack(self.c[source])

        def finish(self):
            for cy in ORDER:
                self.whole(cy).wait_send()

    first = Exchange(o1, c1, es1, er1)
    second = Exchange(o2, c2, es2, er2)

    loads[0].wait()
    loads[1].wait()

    masked = jnp.where(iota((SLOTS, PEERS), 0) < count_ref[...], rows_ref[...], -1)
    code = jnp.concatenate([(masked >> 5).astype(f32), (masked & 31).astype(f32)], axis=0).astype(bf16)

    def outgoing(cy):
        there = (y + cy) % NY
        place = iota((256, PEERS), 0) // 8 + there * PLANE
        spread = jnp.where(iota((256, PEERS), 1) == place, 1.0, 0.0).astype(bf16)
        parts = dot(spread, code, 1, 1)
        lane = iota((256, 16), 1)
        weight = jnp.where(
            (lane & 7) == (iota((256, 16), 0) & 7), jnp.where(lane < 8, 32.0, 1.0), 0.0
        )
        row = jnp.sum(parts * weight, axis=1, keepdims=True).astype(i32)
        hot = jnp.where(iota((256, NODES), 1) == row, 1.0, 0.0).astype(bf16)
        o1[cy] = pack(dot(hot, feat[...]))

    loads[2].wait()
    outgoing(ORDER[0])
    pl.semaphore_wait(barrier, NZ + NX + NY - 2)
    for c in range(1, NX):
        pl.semaphore_signal(x_in, inc=1, device_id=at_x(c), device_id_type=MESH)
    outgoing(ORDER[1])
    pl.semaphore_wait(x_in, NX - 1)
    for c in range(1, NY):
        pl.semaphore_signal(y_in, inc=1, device_id=at_y(c), device_id_type=MESH)
    outgoing(ORDER[2])
    pl.semaphore_wait(y_in, NY - 1)
    for cy in ORDER[:3]:
        first.start(cy)
    outgoing(ORDER[3])
    first.start(ORDER[3])
    swap = remote(target_hbm, other, tsem.at[0], tsem.at[1], mate)
    swap.start()

    for item in loads[3:5]:
        item.wait()

    @pl.loop(0, 8)
    def _(i):
        for j in range(8):
            keep = keep_ref[i, j].astype(f32)
            tile = adj[block(i, 128), j * 128 : (j + 1) * 128].astype(f32)
            adj[block(i, 128), j * 128 : (j + 1) * 128] = (tile * keep).astype(bf16)

    @pl.loop(0, 4)
    def _(r):
        acc[block(r), :] = dot(adj[block(r), :], feat[...])

    loads[5].wait()

    def transpose(source, target):
        @pl.loop(0, 4)
        def _(r):
            for q in range(4):
                target[q * 256 : (q + 1) * 256, block(r)] = source[
                    block(r), q * 256 : (q + 1) * 256
                ].T

    transpose(halo, halo_t)
    transpose(adj, adj_t)

    spread = jnp.where(iota((PEERS, NODES), 1) // 8 == iota((PEERS, NODES), 0), 1.0, 0.0).astype(bf16)
    parts = dot(code, spread)
    slot = iota((16, NODES), 0)
    weight = jnp.where((slot & 7) == (iota((16, NODES), 1) & 7), jnp.where(slot < 8, 32.0, 1.0), 0.0)
    row = jnp.sum(parts * weight, axis=0, keepdims=True).astype(i32)

    @pl.loop(0, 4)
    def _(r):
        sel[block(r), :] = jnp.where(iota((256, NODES), 0) + r * 256 == row, 1.0, 0.0).astype(bf16)

    def gather_in(cy):
        source, rows = first.arrived(cy)

        @pl.loop(0, 4)
        def _(r):
            acc[block(r), :] += dot(halo[block(r), block(source)], rows)

    for item in loads[6:]:
        item.wait()
    swap.wait_recv()
    for cy in ORDER:
        gather_in(cy)

    @pl.loop(0, 4)
    def _(r):
        at = block(r)
        agg = acc[at, :].astype(bf16)
        aggr[at, :] = agg
        value, enc_slope = gelu_both(dot(agg, we_ref[...]) + be_ref[...])
        embed = value.astype(bf16)
        emb[at, :] = embed
        value, in_slope = gelu_both(dot(embed, wi_ref[...]) + bi_ref[...])
        hidden = value.astype(bf16)
        hid[at, :] = hidden
        pred = dot(hidden, wo_ref[...])
        goal = other[at, :].astype(f32)
        squares_p = jnp.sum(pred * pred, axis=1, keepdims=True) + 1e-06
        squares_t = jnp.sum(goal * goal, axis=1, keepdims=True) + 1e-06
        over = 1.0 / jnp.sqrt(squares_p * squares_t)
        cosine = jnp.sum(pred * goal, axis=1, keepdims=True) * over
        pg = (
            (-2.0 * loss_scale * over) * goal + (2.0 * loss_scale * cosine / squares_p) * pred
        ).astype(bf16)
        pgrad[at, :] = pg
        hg = (in_slope * dot(pg, wo_ref[...], 1, 1)).astype(bf16)
        hgrad[at, :] = hg
        eg = (enc_slope * dot(hg, wi_ref[...], 1, 1)).astype(bf16)
        egrad[at, :] = eg
        agrad[at, :] = dot(eg, we_ref[...], 1, 1).astype(bf16)

    pairs = (
        (hid, 0, pgrad, 0), (hid, 1, pgrad, 0), (emb, 0, hgrad, 0), (emb, 0, hgrad, 1), (aggr, 0, egrad, 0),
    )
    for i, (left, lq, right, rq) in enumerate(pairs):
        grad = dot(
            left[:, lq * 256 : (lq + 1) * 256], right[:, rq * 256 : (rq + 1) * 256], 0, 0
        )
        gf[i * 512 : i * 512 + 256, :] = grad[:, :128]
        gf[i * 512 + 256 : (i + 1) * 512, :] = grad[:, 128:]
    enc_bias = jnp.sum(egrad[...].astype(f32), axis=0, keepdims=True)
    in_bias = jnp.sum(hgrad[...].astype(f32), axis=0, keepdims=True)
    bias = jnp.concatenate(
        [enc_bias[:, :128], enc_bias[:, 128:]]
        + [in_bias[:, q * 128 : (q + 1) * 128] for q in range(4)]
        + [jnp.zeros((10, 128), f32)],
        axis=0,
    )
    m1[:HALF, :] = gf[block(1 - v, HALF), :].astype(bf16)
    m1[HALF:, :] = bias.astype(bf16)
    across = remote(m1, n1, vs.at[0], vr.at[0], mate)
    across.start()

    def return_rows(cy):
        there = (y + cy) % NY
        o2[cy] = pack(dot(halo_t[block(there), :], agrad[...]))
        second.start(cy)

    return_rows(ORDER[0])
    return_rows(ORDER[1])

    spot = d // NZ
    across.wait_recv()
    bias = (m1[HALF:, :].astype(f32) + n1[HALF:, :].astype(f32)).astype(bf16)

    @pl.loop(0, 16)
    def _(q):
        own = gf[pl.ds(v * HALF + q * PART, PART), :] + n1[pl.ds(q * PART, PART), :].astype(f32)
        ma[q, :PART, :] = own.astype(bf16)
        ma[q, PART:, :] = bias

    @pl.loop(1, 16)
    def _(c):
        remote(ma.at[(spot + c) % 16], na.at[spot], ps.at[0], pr.at[0], at_plane(c)).start()

    na[spot] = ma[spot]
    plane = remote(ma.at[pl.ds(0, 15)], na.at[pl.ds(0, 15)], ps.at[0], pr.at[0], at_plane(1))

    return_rows(ORDER[2])
    return_rows(ORDER[3])

    plane.wait_recv()
    total = sum(na[q].astype(f32) for q in range(16)).astype(bf16)
    for q in range(6):
        me[q] = total[q * 16 : (q + 1) * 16, :]
    me[6:] = jnp.zeros((2, 16, 128), bf16)

    @pl.loop(1, NZ)
    def _(c):
        remote(me.at[(z + c) % NZ], ne.at[z], hs.at[0], hr.at[0], at_z(c)).start()

    ne[z] = me[z]
    to_z = remote(me.at[pl.ds(0, NZ - 1)], ne.at[pl.ds(0, NZ - 1)], hs.at[0], hr.at[0], at_z(1))

    @pl.loop(0, 4)
    def _(r):
        back[block(r), :] = dot(adj_t[block(r), :], agrad[...])

    to_z.wait_recv()
    scale = 1.0 / (2.0 * NODES * PEERS) ** 0.5
    pz[z] = (sum(ne[q].astype(f32) for q in range(NZ)) * scale).astype(bf16)

    @pl.loop(1, NZ)
    def _(c):
        remote(pz.at[z], pz.at[z], hs.at[1], hr.at[1], at_z(c)).start()

    from_z = remote(me.at[pl.ds(0, NZ - 1)], pz.at[pl.ds(0, NZ - 1)], hs.at[1], hr.at[1], at_z(1))

    def scatter_in(cy):
        source, rows = second.arrived(cy)

        @pl.loop(0, 4)
        def _(r):
            back[block(r), :] += dot(sel[block(r), block(source)], rows)

    scatter_in(ORDER[0])
    from_z.wait_recv()
    for q in range(5):
        pf[v, spot, q * 16 : (q + 1) * 16, :] = pz[q]
    tiny_ref[...] = pz[5].astype(f32)

    @pl.loop(1, 16)
    def _(c):
        remote(pf.at[v, spot], pf.at[v, spot], ps.at[1], pr.at[1], at_plane(c)).start()

    shared = remote(pf.at[v, pl.ds(0, 15)], pf.at[v, pl.ds(0, 15)], ps.at[1], pr.at[1], at_plane(1))
    for cy in ORDER[1:]:
        scatter_in(cy)
    fg_ref[...] = back[...].astype(bf16)
    shared.wait_recv()
    share = remote(pf.at[v], pf.at[v], vs.at[1], vr.at[1], mate)
    share.start()
    remote(pf.at[v], pf.at[1 - v], vs.at[1], vr.at[1], mate).wait_recv()

    swap.wait_send()
    first.finish()
    second.finish()
    for item in (across, plane, to_z, from_z, shared, share):
        item.wait_send()


def results(fg_in, pf, tiny, fg_ref, ew_ref, eb_ref, iw_ref, ib_ref, ow_ref):
    fg_ref[...] = fg_in[...]

    def rows(i):
        return pf[i * 256 : (i + 1) * 256, :].astype(f32)

    for i in range(2):
        for q in range(2):
            ow_ref[i * 256 : (i + 1) * 256, q * 128 : (q + 1) * 128] = rows(2 * i + q)
            col = i * 256 + q * 128
            iw_ref[:, col : col + 128] = rows(4 + 2 * i + q)
    for q in range(2):
        ew_ref[:, q * 128 : (q + 1) * 128] = rows(8 + q)
        eb_ref[:, q * 128 : (q + 1) * 128] = tiny[q : q + 1, :]
    for q in range(4):
        ib_ref[:, q * 128 : (q + 1) * 128] = tiny[2 + q : 3 + q, :]


def local(
    features, local_adjacency, tile_keep, halo_adjacency, send_rows, send_count, target,
    w_encoder, b_encoder, w_predict_in, b_predict_in, w_predict_out,
):
    vmem = pl.BlockSpec(memory_space=pltpu.VMEM)
    anywhere = pl.BlockSpec(memory_space=pl.ANY)
    dma = pltpu.SemaphoreType.DMA
    v16 = lambda *shape: pltpu.VMEM(shape, bf16)
    v32 = lambda *shape: pltpu.VMEM(shape, f32)
    feature_grad, pf, tiny = pl.pallas_call(
        kernel,
        out_shape=(
            jax.ShapeDtypeStruct((NODES, WIDE), bf16),
            jax.ShapeDtypeStruct((2, 16, PART, 128), bf16),
            jax.ShapeDtypeStruct((TINY, 128), f32),
        ),
        in_specs=[anywhere] * 12,
        out_specs=(vmem,) * 3,
        scratch_shapes=[
            v16(NODES, WIDE), v16(NODES, NODES), pltpu.SMEM((8, 8), i32), v16(NODES, NODES),
            pltpu.VMEM((SLOTS, PEERS), i32), pltpu.VMEM((1, PEERS), i32),
            v16(WIDE, WIDE), v32(1, WIDE), v16(WIDE, 2 * WIDE), v32(1, 2 * WIDE), v16(2 * WIDE, WIDE),
            v16(NODES, WIDE), v16(NODES, NODES), v16(NODES, NODES), v16(NODES, NODES),
            v32(NODES, WIDE), v16(NODES, WIDE), v16(NODES, WIDE), v16(NODES, 2 * WIDE),
            v16(NODES, WIDE), v16(NODES, 2 * WIDE), v16(NODES, WIDE), v16(NODES, WIDE), v32(NODES, WIDE),
        ]
        + [v16(NY, PLANE, 16, 128)] * 4
        + [
            v32(2 * HALF, 128), v16(HALF + TINY, 128), v16(HALF + TINY, 128),
            v16(16, PART + TINY, 128), v16(16, PART + TINY, 128),
            v16(NZ, 16, 128), v16(NZ, 16, 128), v16(NZ, 16, 128),
            dma((11,)), dma((2,)), pltpu.SemaphoreType.REGULAR, pltpu.SemaphoreType.REGULAR,
        ]
        + [dma((NY,))] * 4
        + [dma((2,))] * 6,
        compiler_params=pltpu.CompilerParams(
            collective_id=0, has_side_effects=True, vmem_limit_bytes=60 * 1024 * 1024
        ),
    )(
        features[0], local_adjacency[0], tile_keep[0], halo_adjacency[0],
        jnp.swapaxes(send_rows[0], 0, 1), send_count, target[0],
        w_encoder, b_encoder[None], w_predict_in, b_predict_in[None], w_predict_out,
    )
    feature_grad, enc, enc_bias, into, in_bias, out = pl.pallas_call(
        results,
        out_shape=(
            jax.ShapeDtypeStruct((NODES, WIDE), bf16),
            jax.ShapeDtypeStruct((WIDE, WIDE), f32),
            jax.ShapeDtypeStruct((1, WIDE), f32),
            jax.ShapeDtypeStruct((WIDE, 2 * WIDE), f32),
            jax.ShapeDtypeStruct((1, 2 * WIDE), f32),
            jax.ShapeDtypeStruct((2 * WIDE, WIDE), f32),
        ),
        in_specs=[vmem] * 3,
        out_specs=(vmem,) * 6,
    )(
        feature_grad, pf.reshape(2 * HALF, 128), tiny
    )
    return feature_grad[None], enc, enc_bias[0], into, in_bias[0], out


def solution(mesh):
    split = P("view", "dom", None)
    return jax.shard_map(
        local,
        mesh=mesh,
        in_specs=(split, split, split, split, split, P("view", "dom"), split, P(), P(), P(), P(), P()),
        out_specs=(split, P(), P(), P(), P(), P()),
        check_vma=False,
    )
```

```python
import jax
import jax.numpy as jnp
from jax import lax
from jax.experimental import pallas as pl
from jax.experimental.pallas import tpu as pltpu
from jax.sharding import PartitionSpec as P

f32, bf16, i32 = jnp.float32, jnp.bfloat16, jnp.int32
NY, NX, NZ = 4, 4, 8
NODES, WIDE, PEERS, SLOTS = 1024, 256, 128, 8
ORDER = (2, 1, 3, 0)
MESH = pl.DeviceIdType.MESH
PLANE = NX * NZ
HALF, PART, TINY = 1280, 40, 16
GROUP = 32
loss_scale = 64.0


def dot(a, b, ca=1, cb=0):
    return lax.dot_general(a, b, (((ca,), (cb,)), ((), ())), preferred_element_type=f32)


def iota(shape, dim):
    return lax.broadcasted_iota(i32, shape, dim)


def gelu_both(v):
    k = 0.7978845608028654
    c = 0.044715
    v2 = v * v
    h = 0.5 + 0.5 * jnp.tanh(v * (k + (k * c) * v2))
    value = v * h
    slope = h + value * (1.0 - h) * (2.0 * k + (6.0 * k * c) * v2)
    return value, slope


def pack(g):
    rows = g.shape[0] // 8
    left = g[:, :128].reshape(rows, 8, 128)
    right = g[:, 128:].reshape(rows, 8, 128)
    return jnp.concatenate([left, right], axis=1).astype(bf16)


def unpack(c):
    rows = c.shape[0]
    wide = c.astype(f32)
    left = wide[:, :8].reshape(rows * 8, 128)
    right = wide[:, 8:].reshape(rows * 8, 128)
    return jnp.concatenate([left, right], axis=1).astype(bf16)


def block(i, size=256):
    return pl.ds(pl.multiple_of(i * size, size), size)


def kernel(
    feat_hbm, adj_hbm, keep_hbm, halo_hbm, rows_hbm, count_hbm, target_hbm,
    we_hbm, be_hbm, wi_hbm, bi_hbm, wo_hbm,
    fg_ref, pf, tiny_ref,
    feat, adj, keep_ref, halo, rows_ref, count_ref, we_ref, be_ref, wi_ref, bi_ref, wo_ref,
    other, adj_t, halo_t, sel,
    acc, aggr, emb, hid, pgrad, hgrad, egrad, agrad, back,
    o1, c1, o2, c2,
    gf, m1, n1, ma, na, me, ne,
    lsem, tsem, z_in,
    es1, er1, es2, er2, vs, vr, gs, gr, ps, pr, hs, hr,
):
    v = lax.axis_index("view")
    d = lax.axis_index("dom")
    z = d % NZ
    x = (d // NZ) % NX
    y = d // (NZ * NX)

    def at_z(c):
        return (v, (y * NX + x) * NZ + (z + c) % NZ)

    def at_x(c):
        return (v, (y * NX + (x + c) % NX) * NZ + z)

    def at_y(c):
        return (v, (((y + c) % NY) * NX + x) * NZ + z)

    def at_plane(c):
        return (v, (d + c * NZ) % PEERS)

    mate = (1 - v, d)

    barrier = pltpu.get_barrier_semaphore()
    pl.semaphore_signal(barrier, inc=1, device_id=mate, device_id_type=MESH)
    for c in range(1, 16):
        pl.semaphore_signal(barrier, inc=1, device_id=at_plane(c), device_id_type=MESH)
    for c in range(1, NZ):
        pl.semaphore_signal(barrier, inc=1, device_id=at_z(c), device_id_type=MESH)

    loads = [
        pltpu.make_async_copy(src, dst, lsem.at[i])
        for i, (src, dst) in enumerate((
            (rows_hbm, rows_ref), (count_hbm, count_ref), (feat_hbm, feat),
            (keep_hbm, keep_ref), (adj_hbm, adj), (halo_hbm, halo),
            (we_hbm, we_ref), (be_hbm, be_ref), (wi_hbm, wi_ref), (bi_hbm, bi_ref), (wo_hbm, wo_ref),
        ))
    ]
    for item in loads:
        item.start()

    def remote(src, dst, ssem, rsem, device):
        return pltpu.make_async_remote_copy(
            src_ref=src, dst_ref=dst, send_sem=ssem, recv_sem=rsem,
            device_id=device, device_id_type=MESH,
        )

    class Exchange:
        def __init__(self, o, c, ss, rs):
            self.o, self.c, self.ss, self.rs = o, c, ss, rs

        def start(self, cy):
            there = (y + cy) % NY
            here = d % PLANE

            @pl.loop(0 if cy else 1, PLANE)
            def _(i):
                j = (here + i) % PLANE
                remote(
                    self.o.at[cy, j], self.c.at[y, here], self.ss.at[cy], self.rs.at[cy], (v, there * PLANE + j)
                ).start()

            if cy == 0:
                self.c[y, here] = self.o[0, here]

        def whole(self, cy):
            source = (y - cy + NY) % NY
            n = PLANE if cy else PLANE - 1
            return remote(
                self.o.at[cy, pl.ds(0, n)], self.c.at[source, pl.ds(0, n)], self.ss.at[cy], self.rs.at[cy], at_y(cy or 1)
            )

        def arrived(self, cy):
            self.whole(cy).wait_recv()
            source = (y - cy + NY) % NY
            return source, unpack(self.c[source])

        def finish(self):
            for cy in ORDER:
                self.whole(cy).wait_send()

    first = Exchange(o1, c1, es1, er1)
    second = Exchange(o2, c2, es2, er2)

    loads[0].wait()
    loads[1].wait()

    masked = jnp.where(iota((SLOTS, PEERS), 0) < count_ref[...], rows_ref[...], -1)
    code = jnp.concatenate([(masked >> 5).astype(f32), (masked & 31).astype(f32)], axis=0).astype(bf16)

    def outgoing(cy):
        there = (y + cy) % NY
        place = iota((256, PEERS), 0) // 8 + there * PLANE
        spread = jnp.where(iota((256, PEERS), 1) == place, 1.0, 0.0).astype(bf16)
        parts = dot(spread, code, 1, 1)
        lane = iota((256, 16), 1)
        weight = jnp.where(
            (lane & 7) == (iota((256, 16), 0) & 7), jnp.where(lane < 8, 32.0, 1.0), 0.0
        )
        row = jnp.sum(parts * weight, axis=1, keepdims=True).astype(i32)
        hot = jnp.where(iota((256, NODES), 1) == row, 1.0, 0.0).astype(bf16)
        o1[cy] = pack(dot(hot, feat[...]))

    loads[2].wait()
    outgoing(ORDER[0])
    pl.semaphore_wait(barrier, NZ + 15)
    for c in range(1, NZ):
        pl.semaphore_signal(z_in, inc=1, device_id=at_z(c), device_id_type=MESH)
    outgoing(ORDER[1])
    pl.semaphore_wait(z_in, NZ - 1)
    for cy in ORDER[:2]:
        first.start(cy)
    for cy in ORDER[2:]:
        outgoing(cy)
        first.start(cy)
    swap = remote(target_hbm, other, tsem.at[0], tsem.at[1], mate)
    swap.start()

    for item in loads[3:5]:
        item.wait()

    @pl.loop(0, 8)
    def _(i):
        for j in range(8):
            keep = keep_ref[i, j].astype(f32)
            tile = adj[block(i, 128), j * 128 : (j + 1) * 128].astype(f32)
            adj[block(i, 128), j * 128 : (j + 1) * 128] = (tile * keep).astype(bf16)

    @pl.loop(0, 4)
    def _(r):
        acc[block(r), :] = dot(adj[block(r), :], feat[...])

    loads[5].wait()

    def transpose(source, target):
        @pl.loop(0, 4)
        def _(r):
            for q in range(4):
                target[q * 256 : (q + 1) * 256, block(r)] = source[
                    block(r), q * 256 : (q + 1) * 256
                ].T

    transpose(halo, halo_t)
    transpose(adj, adj_t)

    spread = jnp.where(iota((PEERS, NODES), 1) // 8 == iota((PEERS, NODES), 0), 1.0, 0.0).astype(bf16)
    parts = dot(code, spread)
    slot = iota((16, NODES), 0)
    weight = jnp.where((slot & 7) == (iota((16, NODES), 1) & 7), jnp.where(slot < 8, 32.0, 1.0), 0.0)
    row = jnp.sum(parts * weight, axis=0, keepdims=True).astype(i32)

    @pl.loop(0, 4)
    def _(r):
        sel[block(r), :] = jnp.where(iota((256, NODES), 0) + r * 256 == row, 1.0, 0.0).astype(bf16)

    def gather_in(cy):
        source, rows = first.arrived(cy)

        @pl.loop(0, 4)
        def _(r):
            acc[block(r), :] += dot(halo[block(r), block(source)], rows)

    for item in loads[6:]:
        item.wait()
    swap.wait_recv()
    for cy in ORDER:
        gather_in(cy)

    @pl.loop(0, 2)
    def _(r):
        at = block(r, 512)
        agg = acc[at, :].astype(bf16)
        aggr[at, :] = agg
        value, enc_slope = gelu_both(dot(agg, we_ref[...]) + be_ref[...])
        embed = value.astype(bf16)
        emb[at, :] = embed
        value, in_slope = gelu_both(dot(embed, wi_ref[...]) + bi_ref[...])
        hidden = value.astype(bf16)
        hid[at, :] = hidden
        pred = dot(hidden, wo_ref[...])
        goal = other[at, :].astype(f32)
        squares_p = jnp.sum(pred * pred, axis=1, keepdims=True) + 1e-06
        squares_t = jnp.sum(goal * goal, axis=1, keepdims=True) + 1e-06
        over = 1.0 / jnp.sqrt(squares_p * squares_t)
        cosine = jnp.sum(pred * goal, axis=1, keepdims=True) * over
        pg = (
            (-2.0 * loss_scale * over) * goal + (2.0 * loss_scale * cosine / squares_p) * pred
        ).astype(bf16)
        pgrad[at, :] = pg
        hg = (in_slope * dot(pg, wo_ref[...], 1, 1)).astype(bf16)
        hgrad[at, :] = hg
        eg = (enc_slope * dot(hg, wi_ref[...], 1, 1)).astype(bf16)
        egrad[at, :] = eg
        agrad[at, :] = dot(eg, we_ref[...], 1, 1).astype(bf16)

    def return_rows(cy):
        there = (y + cy) % NY
        o2[cy] = pack(dot(halo_t[block(there), :], agrad[...]))
        second.start(cy)

    def half_of(view):
        return (
            lambda: dot(hid[:, block(view)], pgrad[...], 0, 0),
            lambda: dot(emb[...], hgrad[:, block(view)], 0, 0),
            lambda: dot(aggr[:, block(view, 128)], egrad[...], 0, 0),
        )

    def column_sums(ref):
        return jnp.sum(ref[...].astype(f32), axis=0, keepdims=True)

    cuts = ((0, 512), (512, 512), (1024, 256 + TINY))

    def across(i):
        part = pl.ds(*cuts[i])
        return remote(m1.at[part], n1.at[part], vs.at[i], vr.at[i], mate)

    for i, grad in enumerate(half_of(1 - v)):
        value = grad().astype(bf16)
        at, n = cuts[i][0], value.shape[0]
        m1[at : at + n, :] = value[:, :128]
        m1[at + n : at + 2 * n, :] = value[:, 128:]
        if i == 2:
            enc_bias, in_bias = column_sums(egrad), column_sums(hgrad)
            bias = jnp.concatenate(
                [enc_bias[:, :128], enc_bias[:, 128:]]
                + [in_bias[:, q * 128 : (q + 1) * 128] for q in range(4)]
                + [jnp.zeros((10, 128), f32)],
                axis=0,
            )
            m1[HALF:, :] = bias.astype(bf16)
        across(i).start()
    for i, grad in enumerate(half_of(v)):
        value = grad()
        at, n = cuts[i][0], value.shape[0]
        gf[at : at + n, :] = value[:, :128]
        gf[at + n : at + 2 * n, :] = value[:, 128:]

    return_rows(ORDER[0])
    return_rows(ORDER[1])
    pair = z % 2
    spot = d // NZ * 2 + pair

    def at_group(q):
        return (v, q // 2 * NZ + (z - pair) + q % 2)

    for i in range(3):
        across(i).wait_recv()
    bias = m1[HALF:, :].astype(f32) + n1[HALF:, :].astype(f32)
    gf[...] += n1[:HALF, :].astype(f32)

    @pl.loop(0, GROUP)
    def _(q):
        own = gf[pl.ds(pl.multiple_of(q * PART, 8), PART), :]
        ma[q] = jnp.concatenate([own, bias[:8, :]], axis=0).astype(bf16)

    @pl.loop(1, GROUP)
    def _(c):
        q = (spot + c) % GROUP
        remote(ma.at[q], na.at[spot], ps.at[0], pr.at[0], at_group(q)).start()

    na[spot] = ma[spot]
    others = pl.ds(0, GROUP - 1)
    group = remote(ma.at[others], na.at[others], ps.at[0], pr.at[0], at_group((spot + 1) % GROUP))

    return_rows(ORDER[2])
    return_rows(ORDER[3])

    @pl.loop(0, 4)
    def _(r):
        back[block(r), :] = dot(adj_t[block(r), :], agrad[...])

    group.wait_recv()

    me[...] = sum(na[q].astype(f32) for q in range(GROUP)).astype(bf16)
    quarter = z // 2

    @pl.loop(1, 4)
    def _(c):
        remote(me, ne.at[quarter], hs.at[0], hr.at[0], at_z(2 * c)).start()

    ne[quarter] = me[...]
    threes = remote(na.at[pl.ds(0, 3)], ne.at[pl.ds(0, 3)], hs.at[0], hr.at[0], at_z(2))

    def scatter_in(cy):
        source, rows = second.arrived(cy)

        @pl.loop(0, 4)
        def _(r):
            back[block(r), :] += dot(sel[block(r), block(source)], rows)

    scatter_in(ORDER[0])
    threes.wait_recv()
    scale = 1.0 / (2.0 * NODES * PEERS) ** 0.5
    total = sum(ne[q].astype(f32) for q in range(4)) * scale
    pf[v, spot] = total.astype(bf16)
    tiny_ref[...] = total[PART:, :]

    row = 2 * NX

    def share(cy, i):
        q = (y + cy) % NY * row + (spot + i) % row
        return remote(pf.at[v, spot], pf.at[v, spot], gs.at[cy], gr.at[cy], at_group(q))

    def shared(cy):
        part = pl.ds((y - cy + NY) % NY * row, row if cy else row - 1)
        return remote(pf.at[v, part], pf.at[v, part], gs.at[cy], gr.at[cy], at_y(cy or 1))

    def passed(cy, view):
        part = pl.ds((y - cy + NY) % NY * row, row)
        return remote(pf.at[v, part], pf.at[view, part], vs.at[3 + cy], vr.at[3 + cy], mate)

    for cy in ORDER:
        for i in range(0 if cy else 1, row):
            share(cy, i).start()
    for cy in ORDER[1:]:
        scatter_in(cy)
    fg_ref[...] = back[...].astype(bf16)
    for cy in (1, 3, 0, 2):
        shared(cy).wait_recv()
        passed(cy, v).start()
    for cy in range(NY):
        passed(cy, 1 - v).wait_recv()

    swap.wait_send()
    first.finish()
    second.finish()
    for item in (group, threes):
        item.wait_send()
    for i in range(3):
        across(i).wait_send()
    for cy in range(NY):
        shared(cy).wait_send()
        passed(cy, v).wait_send()


def results(fg_in, pf, tiny, fg_ref, ew_ref, eb_ref, iw_ref, ib_ref, ow_ref):
    fg_ref[...] = fg_in[...]

    for i in range(2):
        lanes = [slice(q * 128, (q + 1) * 128) for q in range(4)]
        homes = [(ow_ref, i * 256, lanes[q], q * 256, 256) for q in range(2)]
        homes += [(iw_ref, 0, lanes[2 * i + q], 512 + q * 256, 256) for q in range(2)]
        homes += [(ew_ref, i * 128, lanes[q], 1024 + q * 128, 128) for q in range(2)]
        for q in range(GROUP):
            part = pf[i * GROUP + q].astype(f32)
            low = q * PART
            for ref, top, lane, first, count in homes:
                begin, end = max(low, first), min(low + PART, first + count)
                if begin < end:
                    ref[top + begin - first : top + end - first, lane] = part[begin - low : end - low, :]
    for q in range(2):
        eb_ref[:, q * 128 : (q + 1) * 128] = tiny[q : q + 1, :]
    for q in range(4):
        ib_ref[:, q * 128 : (q + 1) * 128] = tiny[2 + q : 3 + q, :]


def local(
    features, local_adjacency, tile_keep, halo_adjacency, send_rows, send_count, target,
    w_encoder, b_encoder, w_predict_in, b_predict_in, w_predict_out,
):
    vmem = pl.BlockSpec(memory_space=pltpu.VMEM)
    anywhere = pl.BlockSpec(memory_space=pl.ANY)
    dma = pltpu.SemaphoreType.DMA
    v16 = lambda *shape: pltpu.VMEM(shape, bf16)
    v32 = lambda *shape: pltpu.VMEM(shape, f32)
    feature_grad, pf, tiny = pl.pallas_call(
        kernel,
        out_shape=(
            jax.ShapeDtypeStruct((NODES, WIDE), bf16),
            jax.ShapeDtypeStruct((2, GROUP, PART + 8, 128), bf16),
            jax.ShapeDtypeStruct((8, 128), f32),
        ),
        in_specs=[anywhere] * 12,
        out_specs=(vmem,) * 3,
        scratch_shapes=[
            v16(NODES, WIDE), v16(NODES, NODES), pltpu.SMEM((8, 8), i32), v16(NODES, NODES),
            pltpu.VMEM((SLOTS, PEERS), i32), pltpu.VMEM((1, PEERS), i32),
            v16(WIDE, WIDE), v32(1, WIDE), v16(WIDE, 2 * WIDE), v32(1, 2 * WIDE), v16(2 * WIDE, WIDE),
            v16(NODES, WIDE), v16(NODES, NODES), v16(NODES, NODES), v16(NODES, NODES),
            v32(NODES, WIDE), v16(NODES, WIDE), v16(NODES, WIDE), v16(NODES, 2 * WIDE),
            v16(NODES, WIDE), v16(NODES, 2 * WIDE), v16(NODES, WIDE), v16(NODES, WIDE), v32(NODES, WIDE),
        ]
        + [v16(NY, PLANE, 16, 128)] * 4
        + [
            v32(HALF, 128), v16(HALF + TINY, 128), v16(HALF + TINY, 128),
            v16(GROUP, PART + 8, 128), v16(GROUP, PART + 8, 128), v16(PART + 8, 128), v16(4, PART + 8, 128),
            dma((11,)), dma((2,)), pltpu.SemaphoreType.REGULAR,
        ]
        + [dma((NY,))] * 4
        + [dma((7,))] * 2 + [dma((NY,))] * 2 + [dma((1,))] * 4,
        compiler_params=pltpu.CompilerParams(
            collective_id=0, has_side_effects=True, vmem_limit_bytes=60 * 1024 * 1024
        ),
    )(
        features[0], local_adjacency[0], tile_keep[0], halo_adjacency[0],
        jnp.swapaxes(send_rows[0], 0, 1), send_count, target[0],
        w_encoder, b_encoder[None], w_predict_in, b_predict_in[None], w_predict_out,
    )
    feature_grad, enc, enc_bias, into, in_bias, out = pl.pallas_call(
        results,
        out_shape=(
            jax.ShapeDtypeStruct((NODES, WIDE), bf16),
            jax.ShapeDtypeStruct((WIDE, WIDE), f32),
            jax.ShapeDtypeStruct((1, WIDE), f32),
            jax.ShapeDtypeStruct((WIDE, 2 * WIDE), f32),
            jax.ShapeDtypeStruct((1, 2 * WIDE), f32),
            jax.ShapeDtypeStruct((2 * WIDE, WIDE), f32),
        ),
        in_specs=[vmem] * 3,
        out_specs=(vmem,) * 6,
    )(
        feature_grad, pf.reshape(2 * GROUP, PART + 8, 128), tiny
    )
    return feature_grad[None], enc, enc_bias[0], into, in_bias[0], out


def solution(mesh):
    split = P("view", "dom", None)
    return jax.shard_map(
        local,
        mesh=mesh,
        in_specs=(split, split, split, split, split, P("view", "dom"), split, P(), P(), P(), P(), P()),
        out_specs=(split, P(), P(), P(), P(), P()),
        check_vma=False,
    )
```

```python
import jax
import jax.numpy as jnp
from jax import lax
from jax.experimental import pallas as pl
from jax.experimental.pallas import tpu as pltpu
from jax.sharding import PartitionSpec as P

f32, bf16, i32 = jnp.float32, jnp.bfloat16, jnp.int32
NY, NX, NZ = 4, 4, 8
NODES, WIDE, PEERS, SLOTS = 1024, 256, 128, 8
ORDER = (2, 1, 3, 0)
MESH = pl.DeviceIdType.MESH
PLANE = NX * NZ
HALF, PART, TINY = 1280, 40, 16
GROUP = 32
loss_scale = 64.0


def dot(a, b, ca=1, cb=0):
    return lax.dot_general(a, b, (((ca,), (cb,)), ((), ())), preferred_element_type=f32)


def iota(shape, dim):
    return lax.broadcasted_iota(i32, shape, dim)


def gelu_both(v):
    k = 0.7978845608028654
    c = 0.044715
    v2 = v * v
    h = 0.5 + 0.5 * jnp.tanh(v * (k + (k * c) * v2))
    value = v * h
    slope = h + value * (1.0 - h) * (2.0 * k + (6.0 * k * c) * v2)
    return value, slope


def pack(g):
    rows = g.shape[0] // 8
    left = g[:, :128].reshape(rows, 8, 128)
    right = g[:, 128:].reshape(rows, 8, 128)
    return jnp.concatenate([left, right], axis=1).astype(bf16)


def unpack(c):
    rows = c.shape[0]
    wide = c.astype(f32)
    left = wide[:, :8].reshape(rows * 8, 128)
    right = wide[:, 8:].reshape(rows * 8, 128)
    return jnp.concatenate([left, right], axis=1).astype(bf16)


def block(i, size=256):
    return pl.ds(pl.multiple_of(i * size, size), size)


def kernel(
    feat_hbm, adj_hbm, keep_hbm, halo_hbm, rows_hbm, count_hbm, target_hbm,
    we_hbm, be_hbm, wi_hbm, bi_hbm, wo_hbm,
    fg_ref, pf, tiny_ref,
    feat, adj, keep_ref, halo, rows_ref, count_ref, we_ref, be_ref, wi_ref, bi_ref, wo_ref,
    other, adj_t, halo_t, sel,
    acc, aggr, emb, hid, pgrad, hgrad, egrad, agrad, back,
    o1, c1, o2, c2,
    gf, m1, n1, ma, na, me, ne,
    lsem, tsem, z_in,
    es1, er1, es2, er2, vs, vr, gs, gr, ps, pr, hs, hr,
):
    v = lax.axis_index("view")
    d = lax.axis_index("dom")
    z = d % NZ
    x = (d // NZ) % NX
    y = d // (NZ * NX)

    def at_z(c):
        return (v, (y * NX + x) * NZ + (z + c) % NZ)

    def at_x(c):
        return (v, (y * NX + (x + c) % NX) * NZ + z)

    def at_y(c):
        return (v, (((y + c) % NY) * NX + x) * NZ + z)

    def at_plane(c):
        return (v, (d + c * NZ) % PEERS)

    mate = (1 - v, d)

    barrier = pltpu.get_barrier_semaphore()
    pl.semaphore_signal(barrier, inc=1, device_id=mate, device_id_type=MESH)
    for c in range(1, 16):
        pl.semaphore_signal(barrier, inc=1, device_id=at_plane(c), device_id_type=MESH)
    for c in range(1, NZ):
        pl.semaphore_signal(barrier, inc=1, device_id=at_z(c), device_id_type=MESH)

    loads = [
        pltpu.make_async_copy(src, dst, lsem.at[i])
        for i, (src, dst) in enumerate((
            (rows_hbm, rows_ref), (count_hbm, count_ref), (feat_hbm, feat),
            (keep_hbm, keep_ref), (adj_hbm, adj), (halo_hbm, halo),
            (we_hbm, we_ref), (be_hbm, be_ref), (wi_hbm, wi_ref), (bi_hbm, bi_ref), (wo_hbm, wo_ref),
        ))
    ]
    for item in loads:
        item.start()

    def remote(src, dst, ssem, rsem, device):
        return pltpu.make_async_remote_copy(
            src_ref=src, dst_ref=dst, send_sem=ssem, recv_sem=rsem,
            device_id=device, device_id_type=MESH,
        )

    class Exchange:
        def __init__(self, o, c, ss, rs):
            self.o, self.c, self.ss, self.rs = o, c, ss, rs

        def start(self, cy):
            there = (y + cy) % NY
            here = d % PLANE

            @pl.loop(0 if cy else 1, PLANE)
            def _(i):
                j = (here + i) % PLANE
                remote(
                    self.o.at[cy, j], self.c.at[y, here], self.ss.at[cy], self.rs.at[cy], (v, there * PLANE + j)
                ).start()

            if cy == 0:
                self.c[y, here] = self.o[0, here]

        def whole(self, cy):
            source = (y - cy + NY) % NY
            n = PLANE if cy else PLANE - 1
            return remote(
                self.o.at[cy, pl.ds(0, n)], self.c.at[source, pl.ds(0, n)], self.ss.at[cy], self.rs.at[cy], at_y(cy or 1)
            )

        def arrived(self, cy):
            self.whole(cy).wait_recv()
            source = (y - cy + NY) % NY
            return source, unpack(self.c[source])

        def finish(self):
            for cy in ORDER:
                self.whole(cy).wait_send()

    first = Exchange(o1, c1, es1, er1)
    second = Exchange(o2, c2, es2, er2)

    loads[0].wait()
    loads[1].wait()

    masked = jnp.where(iota((SLOTS, PEERS), 0) < count_ref[...], rows_ref[...], -1)
    code = jnp.concatenate([(masked >> 5).astype(f32), (masked & 31).astype(f32)], axis=0).astype(bf16)

    def outgoing(cy):
        there = (y + cy) % NY
        place = iota((256, PEERS), 0) // 8 + there * PLANE
        spread = jnp.where(iota((256, PEERS), 1) == place, 1.0, 0.0).astype(bf16)
        parts = dot(spread, code, 1, 1)
        lane = iota((256, 16), 1)
        weight = jnp.where(
            (lane & 7) == (iota((256, 16), 0) & 7), jnp.where(lane < 8, 32.0, 1.0), 0.0
        )
        row = jnp.sum(parts * weight, axis=1, keepdims=True).astype(i32)
        hot = jnp.where(iota((256, NODES), 1) == row, 1.0, 0.0).astype(bf16)
        o1[cy] = pack(dot(hot, feat[...]))

    loads[2].wait()
    outgoing(ORDER[0])
    pl.semaphore_wait(barrier, NZ + 15)
    for c in range(1, NZ):
        pl.semaphore_signal(z_in, inc=1, device_id=at_z(c), device_id_type=MESH)
    outgoing(ORDER[1])
    pl.semaphore_wait(z_in, NZ - 1)
    for cy in ORDER[:2]:
        first.start(cy)
    for cy in ORDER[2:]:
        outgoing(cy)
        first.start(cy)
    swap = remote(target_hbm, other, tsem.at[0], tsem.at[1], mate)
    swap.start()

    for item in loads[3:5]:
        item.wait()

    @pl.loop(0, 8)
    def _(i):
        for j in range(8):
            keep = keep_ref[i, j].astype(f32)
            tile = adj[block(i, 128), j * 128 : (j + 1) * 128].astype(f32)
            adj[block(i, 128), j * 128 : (j + 1) * 128] = (tile * keep).astype(bf16)

    @pl.loop(0, 4)
    def _(r):
        acc[block(r), :] = dot(adj[block(r), :], feat[...])

    loads[5].wait()

    def transpose(source, target):
        @pl.loop(0, 4)
        def _(r):
            for q in range(4):
                target[q * 256 : (q + 1) * 256, block(r)] = source[
                    block(r), q * 256 : (q + 1) * 256
                ].T

    transpose(halo, halo_t)
    transpose(adj, adj_t)

    spread = jnp.where(iota((PEERS, NODES), 1) // 8 == iota((PEERS, NODES), 0), 1.0, 0.0).astype(bf16)
    parts = dot(code, spread)
    slot = iota((16, NODES), 0)
    weight = jnp.where((slot & 7) == (iota((16, NODES), 1) & 7), jnp.where(slot < 8, 32.0, 1.0), 0.0)
    row = jnp.sum(parts * weight, axis=0, keepdims=True).astype(i32)

    @pl.loop(0, 4)
    def _(r):
        sel[block(r), :] = jnp.where(iota((256, NODES), 0) + r * 256 == row, 1.0, 0.0).astype(bf16)

    def gather_in(cy):
        source, rows = first.arrived(cy)

        acc[...] += dot(halo[:, block(source)], rows)

    for item in loads[6:]:
        item.wait()
    swap.wait_recv()
    for cy in ORDER:
        gather_in(cy)

    @pl.loop(0, 1)
    def _(r):
        at = block(r, NODES)
        agg = acc[at, :].astype(bf16)
        aggr[at, :] = agg
        value, enc_slope = gelu_both(dot(agg, we_ref[...]) + be_ref[...])
        embed = value.astype(bf16)
        emb[at, :] = embed
        value, in_slope = gelu_both(dot(embed, wi_ref[...]) + bi_ref[...])
        hidden = value.astype(bf16)
        hid[at, :] = hidden
        pred = dot(hidden, wo_ref[...])
        goal = other[at, :].astype(f32)
        squares_p = jnp.sum(pred * pred, axis=1, keepdims=True) + 1e-06
        squares_t = jnp.sum(goal * goal, axis=1, keepdims=True) + 1e-06
        over = 1.0 / jnp.sqrt(squares_p * squares_t)
        cosine = jnp.sum(pred * goal, axis=1, keepdims=True) * over
        pg = (
            (-2.0 * loss_scale * over) * goal + (2.0 * loss_scale * cosine / squares_p) * pred
        ).astype(bf16)
        pgrad[at, :] = pg
        hg = (in_slope * dot(pg, wo_ref[...], 1, 1)).astype(bf16)
        hgrad[at, :] = hg
        eg = (enc_slope * dot(hg, wi_ref[...], 1, 1)).astype(bf16)
        egrad[at, :] = eg
        agrad[at, :] = dot(eg, we_ref[...], 1, 1).astype(bf16)

    def return_rows(cy):
        there = (y + cy) % NY
        o2[cy] = pack(dot(halo_t[block(there), :], agrad[...]))
        second.start(cy)

    def half_of(view):
        return (
            lambda: dot(hid[:, block(view)], pgrad[...], 0, 0),
            lambda: dot(emb[...], hgrad[:, block(view)], 0, 0),
            lambda: dot(aggr[:, block(view, 128)], egrad[...], 0, 0),
        )

    def column_sums(ref):
        return jnp.sum(ref[...].astype(f32), axis=0, keepdims=True)

    cuts = ((0, 512), (512, 512), (1024, 256 + TINY))

    def across(i):
        part = pl.ds(*cuts[i])
        return remote(m1.at[part], n1.at[part], vs.at[i], vr.at[i], mate)

    for i, grad in enumerate(half_of(1 - v)):
        value = grad().astype(bf16)
        at, n = cuts[i][0], value.shape[0]
        m1[at : at + n, :] = value[:, :128]
        m1[at + n : at + 2 * n, :] = value[:, 128:]
        if i == 2:
            enc_bias, in_bias = column_sums(egrad), column_sums(hgrad)
            bias = jnp.concatenate(
                [enc_bias[:, :128], enc_bias[:, 128:]]
                + [in_bias[:, q * 128 : (q + 1) * 128] for q in range(4)]
                + [jnp.zeros((10, 128), f32)],
                axis=0,
            )
            m1[HALF:, :] = bias.astype(bf16)
        across(i).start()
    for i, grad in enumerate(half_of(v)):
        value = grad()
        at, n = cuts[i][0], value.shape[0]
        gf[at : at + n, :] = value[:, :128]
        gf[at + n : at + 2 * n, :] = value[:, 128:]

    return_rows(ORDER[0])
    pair = z % 2
    spot = d // NZ * 2 + pair

    def at_group(q):
        return (v, q // 2 * NZ + (z - pair) + q % 2)

    for i in range(3):
        across(i).wait_recv()
    bias = m1[HALF:, :].astype(f32) + n1[HALF:, :].astype(f32)
    gf[...] += n1[:HALF, :].astype(f32)

    def part(q):
        own = gf[pl.ds(pl.multiple_of(q * PART, 8), PART), :]
        return jnp.concatenate([own, bias[:8, :]], axis=0).astype(bf16)

    @pl.loop(1, GROUP)
    def _(c):
        q = (spot + c) % GROUP
        ma[q] = part(q)
        remote(ma.at[q], na.at[spot], ps.at[0], pr.at[0], at_group(q)).start()

    na[spot] = part(spot)
    others = pl.ds(0, GROUP - 1)
    group = remote(ma.at[others], na.at[others], ps.at[0], pr.at[0], at_group((spot + 1) % GROUP))

    return_rows(ORDER[1])
    return_rows(ORDER[2])

    @pl.loop(0, 4)
    def _(r):
        back[block(r), :] = dot(adj_t[block(r), :], agrad[...])

    group.wait_recv()

    me[...] = sum(na[q].astype(f32) for q in range(GROUP)).astype(bf16)
    quarter = z // 2

    @pl.loop(1, 4)
    def _(c):
        remote(me, ne.at[quarter], hs.at[0], hr.at[0], at_z(2 * c)).start()

    ne[quarter] = me[...]
    threes = remote(na.at[pl.ds(0, 3)], ne.at[pl.ds(0, 3)], hs.at[0], hr.at[0], at_z(2))
    return_rows(ORDER[3])

    def scatter_in(cy):
        source, rows = second.arrived(cy)

        back[...] += dot(sel[:, block(source)], rows)

    scatter_in(ORDER[0])
    threes.wait_recv()
    scale = 1.0 / (2.0 * NODES * PEERS) ** 0.5
    total = sum(ne[q].astype(f32) for q in range(4)) * scale
    pf[v, spot] = total.astype(bf16)
    tiny_ref[...] = total[PART:, :]

    row = 2 * NX

    def share(cy, i):
        q = (y + cy) % NY * row + (spot + i) % row
        return remote(pf.at[v, spot], pf.at[v, spot], gs.at[cy], gr.at[cy], at_group(q))

    def shared(cy):
        part = pl.ds((y - cy + NY) % NY * row, row if cy else row - 1)
        return remote(pf.at[v, part], pf.at[v, part], gs.at[cy], gr.at[cy], at_y(cy or 1))

    def passed(cy, view):
        part = pl.ds((y - cy + NY) % NY * row, row)
        return remote(pf.at[v, part], pf.at[view, part], vs.at[3 + cy], vr.at[3 + cy], mate)

    for cy in ORDER:
        for i in range(0 if cy else 1, row):
            share(cy, i).start()
    for cy in ORDER[1:]:
        scatter_in(cy)
    fg_ref[...] = back[...].astype(bf16)
    for cy in (1, 3, 0, 2):
        shared(cy).wait_recv()
        passed(cy, v).start()
    for cy in range(NY):
        passed(cy, 1 - v).wait_recv()

    swap.wait_send()
    first.finish()
    second.finish()
    for item in (group, threes):
        item.wait_send()
    for i in range(3):
        across(i).wait_send()
    for cy in range(NY):
        shared(cy).wait_send()
        passed(cy, v).wait_send()


def results(fg_in, pf, tiny, fg_ref, ew_ref, eb_ref, iw_ref, ib_ref, ow_ref):
    fg_ref[...] = fg_in[...]

    for i in range(2):
        lanes = [slice(q * 128, (q + 1) * 128) for q in range(4)]
        homes = [(ow_ref, i * 256, lanes[q], q * 256, 256) for q in range(2)]
        homes += [(iw_ref, 0, lanes[2 * i + q], 512 + q * 256, 256) for q in range(2)]
        homes += [(ew_ref, i * 128, lanes[q], 1024 + q * 128, 128) for q in range(2)]
        for q in range(GROUP):
            part = pf[i * GROUP + q].astype(f32)
            low = q * PART
            for ref, top, lane, first, count in homes:
                begin, end = max(low, first), min(low + PART, first + count)
                if begin < end:
                    ref[top + begin - first : top + end - first, lane] = part[begin - low : end - low, :]
    for q in range(2):
        eb_ref[:, q * 128 : (q + 1) * 128] = tiny[q : q + 1, :]
    for q in range(4):
        ib_ref[:, q * 128 : (q + 1) * 128] = tiny[2 + q : 3 + q, :]


def local(
    features, local_adjacency, tile_keep, halo_adjacency, send_rows, send_count, target,
    w_encoder, b_encoder, w_predict_in, b_predict_in, w_predict_out,
):
    vmem = pl.BlockSpec(memory_space=pltpu.VMEM)
    anywhere = pl.BlockSpec(memory_space=pl.ANY)
    dma = pltpu.SemaphoreType.DMA
    v16 = lambda *shape: pltpu.VMEM(shape, bf16)
    v32 = lambda *shape: pltpu.VMEM(shape, f32)
    feature_grad, pf, tiny = pl.pallas_call(
        kernel,
        out_shape=(
            jax.ShapeDtypeStruct((NODES, WIDE), bf16),
            jax.ShapeDtypeStruct((2, GROUP, PART + 8, 128), bf16),
            jax.ShapeDtypeStruct((8, 128), f32),
        ),
        in_specs=[anywhere] * 12,
        out_specs=(vmem,) * 3,
        scratch_shapes=[
            v16(NODES, WIDE), v16(NODES, NODES), pltpu.SMEM((8, 8), i32), v16(NODES, NODES),
            pltpu.VMEM((SLOTS, PEERS), i32), pltpu.VMEM((1, PEERS), i32),
            v16(WIDE, WIDE), v32(1, WIDE), v16(WIDE, 2 * WIDE), v32(1, 2 * WIDE), v16(2 * WIDE, WIDE),
            v16(NODES, WIDE), v16(NODES, NODES), v16(NODES, NODES), v16(NODES, NODES),
            v32(NODES, WIDE), v16(NODES, WIDE), v16(NODES, WIDE), v16(NODES, 2 * WIDE),
            v16(NODES, WIDE), v16(NODES, 2 * WIDE), v16(NODES, WIDE), v16(NODES, WIDE), v32(NODES, WIDE),
        ]
        + [v16(NY, PLANE, 16, 128)] * 4
        + [
            v32(HALF, 128), v16(HALF + TINY, 128), v16(HALF + TINY, 128),
            v16(GROUP, PART + 8, 128), v16(GROUP, PART + 8, 128), v16(PART + 8, 128), v16(4, PART + 8, 128),
            dma((11,)), dma((2,)), pltpu.SemaphoreType.REGULAR,
        ]
        + [dma((NY,))] * 4
        + [dma((7,))] * 2 + [dma((NY,))] * 2 + [dma((1,))] * 4,
        compiler_params=pltpu.CompilerParams(
            collective_id=0, has_side_effects=True, vmem_limit_bytes=60 * 1024 * 1024
        ),
    )(
        features[0], local_adjacency[0], tile_keep[0], halo_adjacency[0],
        jnp.swapaxes(send_rows[0], 0, 1), send_count, target[0],
        w_encoder, b_encoder[None], w_predict_in, b_predict_in[None], w_predict_out,
    )
    feature_grad, enc, enc_bias, into, in_bias, out = pl.pallas_call(
        results,
        out_shape=(
            jax.ShapeDtypeStruct((NODES, WIDE), bf16),
            jax.ShapeDtypeStruct((WIDE, WIDE), f32),
            jax.ShapeDtypeStruct((1, WIDE), f32),
            jax.ShapeDtypeStruct((WIDE, 2 * WIDE), f32),
            jax.ShapeDtypeStruct((1, 2 * WIDE), f32),
            jax.ShapeDtypeStruct((2 * WIDE, WIDE), f32),
        ),
        in_specs=[vmem] * 3,
        out_specs=(vmem,) * 6,
    )(
        feature_grad, pf.reshape(2 * GROUP, PART + 8, 128), tiny
    )
    return feature_grad[None], enc, enc_bias[0], into, in_bias[0], out


def solution(mesh):
    split = P("view", "dom", None)
    return jax.shard_map(
        local,
        mesh=mesh,
        in_specs=(split, split, split, split, split, P("view", "dom"), split, P(), P(), P(), P(), P()),
        out_specs=(split, P(), P(), P(), P(), P()),
        check_vma=False,
    )
```

```python
import jax
import jax.numpy as jnp
from jax import lax
from jax.experimental import pallas as pl
from jax.experimental.pallas import tpu as pltpu
from jax.sharding import PartitionSpec as P

f32, bf16, i32 = jnp.float32, jnp.bfloat16, jnp.int32
NY, NX, NZ = 4, 4, 8
NODES, WIDE, PEERS, SLOTS = 1024, 256, 128, 8
ORDER = (2, 1, 3, 0)
MESH = pl.DeviceIdType.MESH
PLANE = NX * NZ
HALF, PART, TINY = 1280, 40, 16
GROUP = 32
loss_scale = 64.0


def dot(a, b, ca=1, cb=0):
    return lax.dot_general(a, b, (((ca,), (cb,)), ((), ())), preferred_element_type=f32)


def iota(shape, dim):
    return lax.broadcasted_iota(i32, shape, dim)


def gelu_both(v):
    k = 0.7978845608028654
    c = 0.044715
    v2 = v * v
    h = 0.5 + 0.5 * jnp.tanh(v * (k + (k * c) * v2))
    value = v * h
    slope = h + value * (1.0 - h) * (2.0 * k + (6.0 * k * c) * v2)
    return value, slope


def pack(g):
    rows = g.shape[0] // 8
    left = g[:, :128].reshape(rows, 8, 128)
    right = g[:, 128:].reshape(rows, 8, 128)
    return jnp.concatenate([left, right], axis=1).astype(bf16)


def unpack(c):
    rows = c.shape[0]
    wide = c.astype(f32)
    left = wide[:, :8].reshape(rows * 8, 128)
    right = wide[:, 8:].reshape(rows * 8, 128)
    return jnp.concatenate([left, right], axis=1).astype(bf16)


def block(i, size=256):
    return pl.ds(pl.multiple_of(i * size, size), size)


def kernel(
    feat_hbm, adj_hbm, keep_hbm, halo_hbm, rows_hbm, count_hbm, target_hbm,
    we_hbm, be_hbm, wi_hbm, bi_hbm, wo_hbm,
    fg_ref, pf, tiny_ref,
    feat, adj, keep_ref, halo, rows_ref, count_ref, we_ref, be_ref, wi_ref, bi_ref, wo_ref,
    other, adj_t, halo_t, sel,
    acc, aggr, emb, hid, pgrad, hgrad, egrad, agrad, back,
    o1, c1, o2, c2,
    gf, m1, n1, ma, na, me, ne,
    lsem, tsem, z_in,
    es1, er1, es2, er2, vs, vr, gs, gr, ps, pr, hs, hr,
):
    v = lax.axis_index("view")
    d = lax.axis_index("dom")
    z = d % NZ
    x = (d // NZ) % NX
    y = d // (NZ * NX)

    def at_z(c):
        return (v, (y * NX + x) * NZ + (z + c) % NZ)

    def at_x(c):
        return (v, (y * NX + (x + c) % NX) * NZ + z)

    def at_y(c):
        return (v, (((y + c) % NY) * NX + x) * NZ + z)

    def at_plane(c):
        return (v, (d + c * NZ) % PEERS)

    mate = (1 - v, d)

    barrier = pltpu.get_barrier_semaphore()
    pl.semaphore_signal(barrier, inc=1, device_id=mate, device_id_type=MESH)
    for c in range(1, 16):
        pl.semaphore_signal(barrier, inc=1, device_id=at_plane(c), device_id_type=MESH)
    for c in range(1, NZ):
        pl.semaphore_signal(barrier, inc=1, device_id=at_z(c), device_id_type=MESH)

    loads = [
        pltpu.make_async_copy(src, dst, lsem.at[i])
        for i, (src, dst) in enumerate((
            (rows_hbm, rows_ref), (count_hbm, count_ref), (feat_hbm, feat),
            (keep_hbm, keep_ref), (adj_hbm, adj), (halo_hbm, halo),
            (we_hbm, we_ref), (be_hbm, be_ref), (wi_hbm, wi_ref), (bi_hbm, bi_ref), (wo_hbm, wo_ref),
        ))
    ]
    for item in loads:
        item.start()

    def remote(src, dst, ssem, rsem, device):
        return pltpu.make_async_remote_copy(
            src_ref=src, dst_ref=dst, send_sem=ssem, recv_sem=rsem,
            device_id=device, device_id_type=MESH,
        )

    class Exchange:
        def __init__(self, o, c, ss, rs):
            self.o, self.c, self.ss, self.rs = o, c, ss, rs

        def start(self, cy):
            there = (y + cy) % NY
            here = d % PLANE

            @pl.loop(0 if cy else 1, PLANE)
            def _(i):
                j = (here + i) % PLANE
                remote(
                    self.o.at[cy, j], self.c.at[y, here], self.ss.at[cy], self.rs.at[cy], (v, there * PLANE + j)
                ).start()

            if cy == 0:
                self.c[y, here] = self.o[0, here]

        def whole(self, cy):
            source = (y - cy + NY) % NY
            n = PLANE if cy else PLANE - 1
            return remote(
                self.o.at[cy, pl.ds(0, n)], self.c.at[source, pl.ds(0, n)], self.ss.at[cy], self.rs.at[cy], at_y(cy or 1)
            )

        def arrived(self, cy):
            self.whole(cy).wait_recv()
            source = (y - cy + NY) % NY
            return source, unpack(self.c[source])

        def finish(self):
            for cy in ORDER:
                self.whole(cy).wait_send()

    first = Exchange(o1, c1, es1, er1)
    second = Exchange(o2, c2, es2, er2)

    loads[0].wait()
    loads[1].wait()

    masked = jnp.where(iota((SLOTS, PEERS), 0) < count_ref[...], rows_ref[...], -1)
    code = jnp.concatenate([(masked >> 5).astype(f32), (masked & 31).astype(f32)], axis=0).astype(bf16)

    def outgoing(cy):
        there = (y + cy) % NY
        place = iota((256, PEERS), 0) // 8 + there * PLANE
        spread = jnp.where(iota((256, PEERS), 1) == place, 1.0, 0.0).astype(bf16)
        parts = dot(spread, code, 1, 1)
        lane = iota((256, 16), 1)
        weight = jnp.where(
            (lane & 7) == (iota((256, 16), 0) & 7), jnp.where(lane < 8, 32.0, 1.0), 0.0
        )
        row = jnp.sum(parts * weight, axis=1, keepdims=True).astype(i32)
        hot = jnp.where(iota((256, NODES), 1) == row, 1.0, 0.0).astype(bf16)
        o1[cy] = pack(dot(hot, feat[...]))

    loads[2].wait()
    outgoing(ORDER[0])
    pl.semaphore_wait(barrier, NZ + 15)
    for c in range(1, NZ):
        pl.semaphore_signal(z_in, inc=1, device_id=at_z(c), device_id_type=MESH)
    outgoing(ORDER[1])
    pl.semaphore_wait(z_in, NZ - 1)
    for cy in ORDER[:2]:
        first.start(cy)
    for cy in ORDER[2:]:
        outgoing(cy)
        first.start(cy)
    swap = remote(target_hbm, other, tsem.at[0], tsem.at[1], mate)
    swap.start()

    for item in loads[3:5]:
        item.wait()

    @pl.loop(0, 8)
    def _(i):
        for j in range(8):
            keep = keep_ref[i, j].astype(f32)
            tile = adj[block(i, 128), j * 128 : (j + 1) * 128].astype(f32)
            adj[block(i, 128), j * 128 : (j + 1) * 128] = (tile * keep).astype(bf16)

    @pl.loop(0, 4)
    def _(r):
        acc[block(r), :] = dot(adj[block(r), :], feat[...])

    loads[5].wait()

    def transpose(source, target):
        @pl.loop(0, 4)
        def _(r):
            for q in range(4):
                target[q * 256 : (q + 1) * 256, block(r)] = source[
                    block(r), q * 256 : (q + 1) * 256
                ].T

    transpose(halo, halo_t)
    def gather_in(cy):
        source, rows = first.arrived(cy)

        acc[...] += dot(halo[:, block(source)], rows)

    for item in loads[6:]:
        item.wait()
    swap.wait_recv()
    for cy in ORDER:
        gather_in(cy)

    @pl.loop(0, 1)
    def _(r):
        at = block(r, NODES)
        agg = acc[at, :].astype(bf16)
        aggr[at, :] = agg
        value, enc_slope = gelu_both(dot(agg, we_ref[...]) + be_ref[...])
        embed = value.astype(bf16)
        emb[at, :] = embed
        value, in_slope = gelu_both(dot(embed, wi_ref[...]) + bi_ref[...])
        hidden = value.astype(bf16)
        hid[at, :] = hidden
        pred = dot(hidden, wo_ref[...])
        goal = other[at, :].astype(f32)
        squares_p = jnp.sum(pred * pred, axis=1, keepdims=True) + 1e-06
        squares_t = jnp.sum(goal * goal, axis=1, keepdims=True) + 1e-06
        over = 1.0 / jnp.sqrt(squares_p * squares_t)
        cosine = jnp.sum(pred * goal, axis=1, keepdims=True) * over
        pg = (
            (-2.0 * loss_scale * over) * goal + (2.0 * loss_scale * cosine / squares_p) * pred
        ).astype(bf16)
        pgrad[at, :] = pg
        hg = (in_slope * dot(pg, wo_ref[...], 1, 1)).astype(bf16)
        hgrad[at, :] = hg
        eg = (enc_slope * dot(hg, wi_ref[...], 1, 1)).astype(bf16)
        egrad[at, :] = eg
        agrad[at, :] = dot(eg, we_ref[...], 1, 1).astype(bf16)

    def return_rows(cy):
        there = (y + cy) % NY
        o2[cy] = pack(dot(halo_t[block(there), :], agrad[...]))
        second.start(cy)

    def half_of(view):
        return (
            lambda: dot(hid[:, block(view)], pgrad[...], 0, 0),
            lambda: dot(emb[...], hgrad[:, block(view)], 0, 0),
            lambda: dot(aggr[:, block(view, 128)], egrad[...], 0, 0),
        )

    def column_sums(ref):
        return jnp.sum(ref[...].astype(f32), axis=0, keepdims=True)

    cuts = ((0, 512), (512, 512), (1024, 256 + TINY))

    def across(i):
        part = pl.ds(*cuts[i])
        return remote(m1.at[part], n1.at[part], vs.at[i], vr.at[i], mate)

    for i, grad in enumerate(half_of(1 - v)):
        value = grad().astype(bf16)
        at, n = cuts[i][0], value.shape[0]
        m1[at : at + n, :] = value[:, :128]
        m1[at + n : at + 2 * n, :] = value[:, 128:]
        if i == 2:
            enc_bias, in_bias = column_sums(egrad), column_sums(hgrad)
            bias = jnp.concatenate(
                [enc_bias[:, :128], enc_bias[:, 128:]]
                + [in_bias[:, q * 128 : (q + 1) * 128] for q in range(4)]
                + [jnp.zeros((10, 128), f32)],
                axis=0,
            )
            m1[HALF:, :] = bias.astype(bf16)
        across(i).start()
    for i, grad in enumerate(half_of(v)):
        value = grad()
        at, n = cuts[i][0], value.shape[0]
        gf[at : at + n, :] = value[:, :128]
        gf[at + n : at + 2 * n, :] = value[:, 128:]

    return_rows(0)
    pair = z % 2
    spot = d // NZ * 2 + pair

    def at_group(q):
        return (v, q // 2 * NZ + (z - pair) + q % 2)

    for i in range(3):
        across(i).wait_recv()
    bias = m1[HALF:, :].astype(f32) + n1[HALF:, :].astype(f32)
    gf[...] += n1[:HALF, :].astype(f32)

    def part(q):
        own = gf[pl.ds(pl.multiple_of(q * PART, 8), PART), :]
        return jnp.concatenate([own, bias[:8, :]], axis=0).astype(bf16)

    @pl.loop(1, GROUP)
    def _(c):
        q = (spot + c) % GROUP
        ma[q] = part(q)
        remote(ma.at[q], na.at[spot], ps.at[0], pr.at[0], at_group(q)).start()

    na[spot] = part(spot)
    others = pl.ds(0, GROUP - 1)
    group = remote(ma.at[others], na.at[others], ps.at[0], pr.at[0], at_group((spot + 1) % GROUP))

    return_rows(3)
    return_rows(1)

    transpose(adj, adj_t)

    spread = jnp.where(iota((PEERS, NODES), 1) // 8 == iota((PEERS, NODES), 0), 1.0, 0.0).astype(bf16)
    parts = dot(code, spread)
    slot = iota((16, NODES), 0)
    weight = jnp.where((slot & 7) == (iota((16, NODES), 1) & 7), jnp.where(slot < 8, 32.0, 1.0), 0.0)
    row = jnp.sum(parts * weight, axis=0, keepdims=True).astype(i32)

    @pl.loop(0, 4)
    def _(r):
        sel[block(r), :] = jnp.where(iota((256, NODES), 0) + r * 256 == row, 1.0, 0.0).astype(bf16)

    @pl.loop(0, 4)
    def _(r):
        back[block(r), :] = dot(adj_t[block(r), :], agrad[...])

    group.wait_recv()

    me[...] = sum(na[q].astype(f32) for q in range(GROUP)).astype(bf16)
    quarter = z // 2

    @pl.loop(1, 4)
    def _(c):
        remote(me, ne.at[quarter], hs.at[0], hr.at[0], at_z(2 * c)).start()

    ne[quarter] = me[...]
    threes = remote(na.at[pl.ds(0, 3)], ne.at[pl.ds(0, 3)], hs.at[0], hr.at[0], at_z(2))
    return_rows(2)

    def scatter_in(cy):
        source, rows = second.arrived(cy)

        back[...] += dot(sel[:, block(source)], rows)

    scatter_in(0)
    threes.wait_recv()
    scale = 1.0 / (2.0 * NODES * PEERS) ** 0.5
    total = sum(ne[q].astype(f32) for q in range(4)) * scale
    pf[v, spot] = total.astype(bf16)
    tiny_ref[...] = total[PART:, :]

    row = 2 * NX

    def share(cy, i):
        q = (y + cy) % NY * row + (spot + i) % row
        return remote(pf.at[v, spot], pf.at[v, spot], gs.at[cy], gr.at[cy], at_group(q))

    def shared(cy):
        part = pl.ds((y - cy + NY) % NY * row, row if cy else row - 1)
        return remote(pf.at[v, part], pf.at[v, part], gs.at[cy], gr.at[cy], at_y(cy or 1))

    def passed(cy, view):
        part = pl.ds((y - cy + NY) % NY * row, row)
        return remote(pf.at[v, part], pf.at[view, part], vs.at[3 + cy], vr.at[3 + cy], mate)

    for cy in ORDER:
        for i in range(0 if cy else 1, row):
            share(cy, i).start()
    for cy in (3, 1, 2):
        scatter_in(cy)
    fg_ref[...] = back[...].astype(bf16)
    for cy in (1, 3, 0, 2):
        shared(cy).wait_recv()
        passed(cy, v).start()
    for cy in range(NY):
        passed(cy, 1 - v).wait_recv()

    swap.wait_send()
    first.finish()
    second.finish()
    for item in (group, threes):
        item.wait_send()
    for i in range(3):
        across(i).wait_send()
    for cy in range(NY):
        shared(cy).wait_send()
        passed(cy, v).wait_send()


def results(fg_in, pf, tiny, fg_ref, ew_ref, eb_ref, iw_ref, ib_ref, ow_ref):
    fg_ref[...] = fg_in[...]

    for i in range(2):
        lanes = [slice(q * 128, (q + 1) * 128) for q in range(4)]
        homes = [(ow_ref, i * 256, lanes[q], q * 256, 256) for q in range(2)]
        homes += [(iw_ref, 0, lanes[2 * i + q], 512 + q * 256, 256) for q in range(2)]
        homes += [(ew_ref, i * 128, lanes[q], 1024 + q * 128, 128) for q in range(2)]
        for q in range(GROUP):
            part = pf[i * GROUP + q].astype(f32)
            low = q * PART
            for ref, top, lane, first, count in homes:
                begin, end = max(low, first), min(low + PART, first + count)
                if begin < end:
                    ref[top + begin - first : top + end - first, lane] = part[begin - low : end - low, :]
    for q in range(2):
        eb_ref[:, q * 128 : (q + 1) * 128] = tiny[q : q + 1, :]
    for q in range(4):
        ib_ref[:, q * 128 : (q + 1) * 128] = tiny[2 + q : 3 + q, :]


def local(
    features, local_adjacency, tile_keep, halo_adjacency, send_rows, send_count, target,
    w_encoder, b_encoder, w_predict_in, b_predict_in, w_predict_out,
):
    vmem = pl.BlockSpec(memory_space=pltpu.VMEM)
    anywhere = pl.BlockSpec(memory_space=pl.ANY)
    dma = pltpu.SemaphoreType.DMA
    v16 = lambda *shape: pltpu.VMEM(shape, bf16)
    v32 = lambda *shape: pltpu.VMEM(shape, f32)
    feature_grad, pf, tiny = pl.pallas_call(
        kernel,
        out_shape=(
            jax.ShapeDtypeStruct((NODES, WIDE), bf16),
            jax.ShapeDtypeStruct((2, GROUP, PART + 8, 128), bf16),
            jax.ShapeDtypeStruct((8, 128), f32),
        ),
        in_specs=[anywhere] * 12,
        out_specs=(vmem,) * 3,
        scratch_shapes=[
            v16(NODES, WIDE), v16(NODES, NODES), pltpu.SMEM((8, 8), i32), v16(NODES, NODES),
            pltpu.VMEM((SLOTS, PEERS), i32), pltpu.VMEM((1, PEERS), i32),
            v16(WIDE, WIDE), v32(1, WIDE), v16(WIDE, 2 * WIDE), v32(1, 2 * WIDE), v16(2 * WIDE, WIDE),
            v16(NODES, WIDE), v16(NODES, NODES), v16(NODES, NODES), v16(NODES, NODES),
            v32(NODES, WIDE), v16(NODES, WIDE), v16(NODES, WIDE), v16(NODES, 2 * WIDE),
            v16(NODES, WIDE), v16(NODES, 2 * WIDE), v16(NODES, WIDE), v16(NODES, WIDE), v32(NODES, WIDE),
        ]
        + [v16(NY, PLANE, 16, 128)] * 4
        + [
            v32(HALF, 128), v16(HALF + TINY, 128), v16(HALF + TINY, 128),
            v16(GROUP, PART + 8, 128), v16(GROUP, PART + 8, 128), v16(PART + 8, 128), v16(4, PART + 8, 128),
            dma((11,)), dma((2,)), pltpu.SemaphoreType.REGULAR,
        ]
        + [dma((NY,))] * 4
        + [dma((7,))] * 2 + [dma((NY,))] * 2 + [dma((1,))] * 4,
        compiler_params=pltpu.CompilerParams(
            collective_id=0, has_side_effects=True, vmem_limit_bytes=60 * 1024 * 1024
        ),
    )(
        features[0], local_adjacency[0], tile_keep[0], halo_adjacency[0],
        jnp.swapaxes(send_rows[0], 0, 1), send_count, target[0],
        w_encoder, b_encoder[None], w_predict_in, b_predict_in[None], w_predict_out,
    )
    feature_grad, enc, enc_bias, into, in_bias, out = pl.pallas_call(
        results,
        out_shape=(
            jax.ShapeDtypeStruct((NODES, WIDE), bf16),
            jax.ShapeDtypeStruct((WIDE, WIDE), f32),
            jax.ShapeDtypeStruct((1, WIDE), f32),
            jax.ShapeDtypeStruct((WIDE, 2 * WIDE), f32),
            jax.ShapeDtypeStruct((1, 2 * WIDE), f32),
            jax.ShapeDtypeStruct((2 * WIDE, WIDE), f32),
        ),
        in_specs=[vmem] * 3,
        out_specs=(vmem,) * 6,
    )(
        feature_grad, pf.reshape(2 * GROUP, PART + 8, 128), tiny
    )
    return feature_grad[None], enc, enc_bias[0], into, in_bias[0], out


def solution(mesh):
    split = P("view", "dom", None)
    return jax.shard_map(
        local,
        mesh=mesh,
        in_specs=(split, split, split, split, split, P("view", "dom"), split, P(), P(), P(), P(), P()),
        out_specs=(split, P(), P(), P(), P(), P()),
        check_vma=False,
    )
```
